512 devices in a mesh: section: 16 (over x, y_hi, core), expert: 32 (over z, y_lo).
Axes of the slice: x: 4, y: 8 (y_hi: 2, y_lo: 4; y = y_hi * 4 + y_lo), z: 8, core: 2. Of those that a mesh axis runs over, the one named last changes fastest.
Arguments:
- hidden_fwd: bfloat16 [16, 2048, 1024], P('section', 'expert'), may hold values from -6 to 6
- hidden_bwd: bfloat16 [16, 2048, 1024], P('section', 'expert'), may hold values from -6 to 6
- mid_bwd: bfloat16 [16, 2048, 1024], P('section', 'expert'), may hold values from -6 to 6
- grads_in: bfloat16 [16, 2048, 1024], P('section', 'expert'), may hold values from -6 to 6
- memory_saved: bfloat16 [2048, 1024], P('expert'), may hold values from -6 to 6
- lengths: int32 [4, 64], P(None, 'expert'), may hold values from 1 to 32
- routes_fwd: int32 [16, 2048, 2], P('section', 'expert'), may hold values from 0 to 3, all different within a row; in each aligned block of 64 rows (0 to 63, 64 to 127, ..., all dimensions but the last counted through in order) at most 36 rows name the same one
- routes_bwd: int32 [16, 2048, 2], P('section', 'expert'), may hold values from 0 to 3, all different within a row; in each aligned block of 64 rows (0 to 63, 64 to 127, ..., all dimensions but the last counted through in order) at most 36 rows name the same one
- probs_fwd: float32 [16, 2048, 2], P('section', 'expert'), may hold values from 0.1 to 0.9
- probs_bwd: float32 [16, 2048, 2], P('section', 'expert'), may hold values from 0.1 to 0.9
- norm_gains: float32 [16, 2, 1024], P('section'), may hold values from 0.5 to 1.5
- w_in: bfloat16 [16, 1024, 16384], P('section', None, 'expert'), may hold values from -0.1875 to 0.1875
- w_out: bfloat16 [16, 16384, 1024], P('section', 'expert'), may hold values from -0.09375 to 0.09375
- w_query: bfloat16 [16, 1024, 512], P('section', 'expert'), may hold values from -0.1875 to 0.1875
- w_keyval: bfloat16 [16, 1024, 1024], P('section', 'expert'), may hold values from -0.1875 to 0.1875
- w_output: bfloat16 [16, 512, 1024], P('section', 'expert'), may hold values from -0.25 to 0.25
Outputs:
- passed_rows: bfloat16 [16, 2048, 1024], P('section', 'expert')
- passed_grads: bfloat16 [16, 2048, 1024], P('section', 'expert')
- memory_grad: bfloat16 [2048, 1024], P('expert')
The draws below stay inside these ranges and needn't reach their ends.
Inputs may be any that keep to these rules, and one draw needn't show every extreme that they name: `routes_fwd`: in the 64 rows of one section and one device no expert is named by more than 36 rows; a row's two experts differ. `routes_bwd`: in the 64 rows of one section and one device no expert is named by more than 36 rows; a row's two experts differ.
All inputs are finite; a program needn't handle non-finite values.
Results may differ from the reference program's by a relative error of at most 0.024.
Values may be sent and summed in bfloat16 or wider, within the bound.
A program may use at most 64 MiB of HBM per device.

```python
import math
import jax
import jax.numpy as jnp
import numpy as np
from jax import lax

D = 1024
FF = 4096
HEAD_DIM = 64
EXPERTS = 4
SEQ = 32
SENTS = 2
INNER = 512
TOK_MB = 64
CAP = 36
ROWS = 2048
N_SECTION = 16
N_EXPERT = 32


def with_ends(values, key, least, largest):
    longest = values.shape.index(max(values.shape))
    spots = []
    for shift in (0, 1):
        where = [jax.random.randint(jax.random.fold_in(key, axis), (), 0, length) for axis, length in enumerate(values.shape)]
        where[longest] = (where[longest] + shift) % values.shape[longest]
        spots.append(tuple(where))
    return values.at[spots[0]].set(least).at[spots[1]].set(largest)


def block_scale(key, dims, shards, least, high):
    loudness, own = 1.0, jax.random.fold_in(key, 6)
    for dim, parts in shards:
        steps = jnp.exp(jax.random.uniform(jax.random.fold_in(own, dim), (parts,), jnp.float32, least / len(shards), high / len(shards)))
        loudness = loudness * jnp.repeat(steps, dims[dim] // parts).reshape([-1 if axis == dim else 1 for axis in range(len(dims))])
    return loudness


def assign_block(stream_key, own, number, rows, count, top, limit, skew):
    sequence = jax.random.permutation(stream_key, count)
    packed, common = load_shares(count, rows * top, limit, skew, True), load_shares(count, rows * top, limit, skew, False)
    places = jnp.arange(count)

    def named(sizes, offset_by):
        used = int((sizes > 0).sum())
        fixed = max(1, used // 4)
        shifted = fixed + (places - fixed + offset_by * (used - fixed)) % max(1, count - fixed)
        return jnp.zeros((count,), jnp.int32).at[sequence[jnp.where(places < fixed, places, shifted)]].set(jnp.asarray(sizes, jnp.int32))

    sizes = jnp.where(number % 4 == 0, named(packed, number // 4), named(common, number - number // 4 - 1))
    mixed = jax.random.permutation(jax.random.fold_in(own, 3), count)
    donor, sink = mixed[0:count // 2 * 2:2], mixed[1:count // 2 * 2:2]
    margin = jnp.minimum(sizes[donor] - 1, limit - sizes[sink]) // 2
    margin = jnp.where((donor == sequence[0]) | (sink == sequence[0]) | (sizes[sink] == 0), 0, jnp.maximum(margin, 0))
    shifted = jax.random.randint(jax.random.fold_in(own, 4), (count // 2,), 0, 1 << 20) % (margin + 1)
    sizes = sizes.at[donor].add(-shifted).at[sink].add(shifted)
    labels = jnp.searchsorted(jnp.cumsum(sizes), jnp.arange(rows * top), side="right").astype(jnp.int32)
    listing = labels.reshape(top, rows).T
    listing = listing[jax.random.permutation(jax.random.fold_in(own, 1), rows)]
    offset_by = jax.random.randint(jax.random.fold_in(own, 2), (rows, 1), 0, top)
    return jnp.take_along_axis(listing, (jnp.arange(top)[None, :] + offset_by) % top, axis=1)


def load_shares(count, total, limit, skew, full):
    weights = [(1 << 20) // math.isqrt(grade ** skew) + 1 for grade in range(1, count + 1)]
    largest = limit if full else min(limit, max(-(-total // count), total * weights[0] // sum(weights)))
    least = 1 if total - largest >= count - 1 else 0
    holding, spare = [largest] + [least] * (count - 1), total - largest - least * (count - 1)
    while spare > 0:
        free = [i for i in range(1, count) if holding[i] < largest] or [i for i in range(1, count) if holding[i] < limit]
        pool, left = sum([weights[i] for i in free]), spare
        for i in free:
            extra = min(limit - holding[i], max(1, left * weights[i] // pool), spare)
            holding[i] = holding[i] + extra
            spare = spare - extra
    return np.array(holding)


def scatter_about(key, extent, width, bound, shards=(), held_as=jnp.bfloat16):
    factor_of = block_scale(key, extent, shards, -0.22, 0.18) if shards else 1.0
    values = jax.random.normal(key, extent, jnp.float32) * width * factor_of
    return jnp.minimum(jnp.maximum(values, -bound), bound).astype(held_as)


def setup_inputs(seed: int = 0) -> dict:
    key_list = jax.random.split(jax.random.key(seed), 17)
    hidden_fwd = scatter_about(key_list[0], (N_SECTION, ROWS, D), 1.0, 6.0, ((0, 16), (1, 32)))
    hidden_bwd = scatter_about(key_list[1], (N_SECTION, ROWS, D), 1.0, 6.0, ((0, 16), (1, 32)))
    mid_bwd = scatter_about(key_list[2], (N_SECTION, ROWS, D), 1.0, 6.0, ((0, 16), (1, 32)))
    grads_in = scatter_about(key_list[3], (N_SECTION, ROWS, D), 1.0, 6.0, ((0, 16), (1, 32)))
    memory_saved = scatter_about(key_list[4], (ROWS, D), 1.0, 6.0, ((0, 32),))
    lengths = with_ends(jax.random.randint(key_list[5], (4, N_EXPERT * SENTS), 1, SEQ + 1), jax.random.fold_in(key_list[5], 1), 1, SEQ).astype(jnp.int32)
    routes_fwd_keys = jax.random.split(jax.random.fold_in(key_list[6], 1), N_SECTION * ROWS // TOK_MB)
    routes_fwd_turns = jax.random.permutation(jax.random.fold_in(key_list[6], 3), N_SECTION * ROWS // TOK_MB)
    routes_fwd = jax.vmap(lambda own, number: assign_block(jax.random.fold_in(key_list[6], 2), own, number, TOK_MB, EXPERTS, 2, CAP, 2))(routes_fwd_keys, routes_fwd_turns).reshape((N_SECTION, ROWS, 2))
    routes_bwd_keys = jax.random.split(jax.random.fold_in(key_list[7], 1), N_SECTION * ROWS // TOK_MB)
    routes_bwd_turns = jax.random.permutation(jax.random.fold_in(key_list[7], 3), N_SECTION * ROWS // TOK_MB)
    routes_bwd = jax.vmap(lambda own, number: assign_block(jax.random.fold_in(key_list[7], 2), own, number, TOK_MB, EXPERTS, 2, CAP, 2))(routes_bwd_keys, routes_bwd_turns).reshape((N_SECTION, ROWS, 2))
    probs_fwd = jnp.clip(0.1 + 0.79999997 * jax.random.uniform(key_list[8], (N_SECTION, ROWS, 2), jnp.float32) ** block_scale(key_list[8], (N_SECTION, ROWS, 2), ((0, 16), (1, 32)), -0.2, 0.2), 0.1, 0.9)
    probs_bwd = jnp.clip(0.1 + 0.79999997 * jax.random.uniform(key_list[9], (N_SECTION, ROWS, 2), jnp.float32) ** block_scale(key_list[9], (N_SECTION, ROWS, 2), ((0, 16), (1, 32)), -0.2, 0.2), 0.1, 0.9)
    norm_gains = jnp.clip(1.0 + 0.1 * jax.random.normal(key_list[10], (N_SECTION, 2, D), jnp.float32), 0.5, 1.5)
    w_in = scatter_about(key_list[11], (N_SECTION, D, EXPERTS * FF), D ** -0.5, 0.1875, ((0, 16), (2, 32)))
    w_out = scatter_about(key_list[12], (N_SECTION, EXPERTS * FF, D), FF ** -0.5, 0.09375, ((0, 16), (1, 32)))
    w_query = scatter_about(key_list[13], (N_SECTION, D, INNER), D ** -0.5, 0.1875, ((0, 16), (1, 32)))
    w_keyval = scatter_about(key_list[14], (N_SECTION, D, 2 * INNER), D ** -0.5, 0.1875, ((0, 16), (1, 32)))
    w_output = scatter_about(key_list[15], (N_SECTION, INNER, D), INNER ** -0.5, 0.25, ((0, 16), (1, 32)))
    return {"hidden_fwd": hidden_fwd, "hidden_bwd": hidden_bwd, "mid_bwd": mid_bwd, "grads_in": grads_in, "memory_saved": memory_saved, "lengths": lengths, "routes_fwd": routes_fwd, "routes_bwd": routes_bwd, "probs_fwd": probs_fwd, "probs_bwd": probs_bwd, "norm_gains": norm_gains, "w_in": w_in, "w_out": w_out, "w_query": w_query, "w_keyval": w_keyval, "w_output": w_output}


EPS = 1e-05
ROOT_HALF = 0.7071067811865476
INV_ROOT_TWO_PI = 0.3989422804014327

def layer_norm(row_block, gain_row):
    values = row_block.astype(jnp.float32)
    center = values - lax.optimization_barrier(jnp.mean(values, axis=-1, keepdims=True))
    spread = lax.optimization_barrier(jnp.mean(center * center, axis=-1, keepdims=True))
    return center * lax.rsqrt(spread + EPS) * gain_row

def gelu_value(inputs):
    return 0.5 * inputs * (1.0 + lax.erf(inputs * ROOT_HALF))

def gelu_slope(inputs):
    return 0.5 * (1.0 + lax.erf(inputs * ROOT_HALF)) + inputs * jnp.exp(-0.5 * inputs * inputs) * INV_ROOT_TWO_PI

def row_lengths(sent_lens, row_count):
    sentence = jnp.arange(row_count) // SEQ
    sent_match = sentence[:, None] == jnp.arange(sent_lens.shape[0])[None, :]
    return lax.optimization_barrier(jnp.sum(jnp.where(sent_match, sent_lens[None, :], 0), axis=1))

def cross_attend(middle, memory, src_len, gain_row, query_w, keyval_w, output_w):
    row_count = middle.shape[0]
    inner_width = query_w.shape[1]
    head_count = inner_width // HEAD_DIM
    normed = layer_norm(middle, gain_row).astype(jnp.bfloat16)
    query_rows = jnp.dot(normed, query_w, preferred_element_type=jnp.float32).astype(jnp.bfloat16)
    keyval = jnp.dot(memory, keyval_w, preferred_element_type=jnp.float32).astype(jnp.bfloat16)
    q_heads = query_rows.reshape(row_count, head_count, HEAD_DIM).astype(jnp.float32)
    k_heads = keyval[:, :inner_width].reshape(row_count, head_count, HEAD_DIM).astype(jnp.float32)
    v_heads = keyval[:, inner_width:].reshape(row_count, head_count, HEAD_DIM).astype(jnp.float32)
    scores = jnp.einsum('qhd,khd->hqk', q_heads, k_heads) * HEAD_DIM ** (-0.5)
    row_index = jnp.arange(row_count)
    sentence = row_index // SEQ
    key_len = row_lengths(src_len, row_count)
    allowed = (sentence[:, None] == sentence[None, :]) & ((row_index % SEQ)[None, :] < key_len[None, :])
    raised = jnp.where(allowed[None], jnp.exp(scores), 0.0)
    weights = (raised / lax.optimization_barrier(jnp.sum(raised, axis=-1, keepdims=True))).astype(jnp.bfloat16)
    mixed_heads = jnp.einsum('hqk,khd->qhd', weights.astype(jnp.float32), v_heads).astype(jnp.bfloat16)
    projected = jnp.dot(mixed_heads.reshape(row_count, inner_width), output_w, preferred_element_type=jnp.float32)
    return (middle.astype(jnp.float32) + projected).astype(jnp.bfloat16)

def reference(hidden_fwd, hidden_bwd, mid_bwd, grads_in, memory_saved, lengths, routes_fwd, routes_bwd, probs_fwd, probs_bwd, norm_gains, w_in, w_out, w_query, w_keyval, w_output):
    first_decoder = max(1, 3 * N_SECTION // 16)
    slice_count = N_EXPERT // EXPERTS
    slice_width = FF // slice_count
    position = jnp.arange(ROWS) % SEQ
    section_ids = jnp.arange(N_SECTION)

    def live_rows(sent_lens):
        return (position < row_lengths(sent_lens, ROWS)).astype(jnp.float32)

    def blocks(array):
        return array.reshape(N_EXPERT, TOK_MB, array.shape[-1])

    def expert_mix(normed, routes, probs, live, up_w, down_w):
        total = jnp.zeros((ROWS, D), jnp.float32)
        for expert in range(EXPERTS):
            share = lax.optimization_barrier(jnp.sum(jnp.where(routes == expert, probs, 0.0), axis=1)) * live
            part_sum = jnp.zeros((ROWS, D), jnp.float32)
            for piece in range(slice_count):
                start = expert * FF + piece * slice_width
                units = gelu_value(jnp.dot(normed, up_w[:, start:start + slice_width], preferred_element_type=jnp.float32)).astype(jnp.bfloat16)
                part = jnp.dot(units, down_w[start:start + slice_width], preferred_element_type=jnp.float32).astype(jnp.bfloat16)
                part_sum = part_sum + lax.optimization_barrier(part).astype(jnp.float32)
            total = total + share[:, None] * part_sum
        return total

    def expert_grad(normed, routes, probs, live, upstream, up_w, down_w):
        total = jnp.zeros((ROWS, D), jnp.float32)
        for expert in range(EXPERTS):
            share = lax.optimization_barrier(jnp.sum(jnp.where(routes == expert, probs, 0.0), axis=1)) * live
            sent_rows = (share[:, None] * upstream).astype(jnp.bfloat16)
            for piece in range(slice_count):
                start = expert * FF + piece * slice_width
                up_part = up_w[:, start:start + slice_width]
                down_part = down_w[start:start + slice_width]
                pre_act = jnp.dot(normed, up_part, preferred_element_type=jnp.float32)
                unit_grad = (jnp.dot(sent_rows, down_part.T, preferred_element_type=jnp.float32) * gelu_slope(pre_act)).astype(jnp.bfloat16)
                dpart = jnp.dot(unit_grad, up_part.T, preferred_element_type=jnp.float32).astype(jnp.bfloat16)
                total = total + lax.optimization_barrier(dpart).astype(jnp.float32)
        return total

    def forward_section(items):
        section, hidden, routes, probs, gains, up_w, down_w = items
        sent_lens = jnp.where(section >= first_decoder, lengths[1], lengths[0])
        normed = layer_norm(hidden, gains[0]).astype(jnp.bfloat16)
        mixed = expert_mix(normed, routes, probs, live_rows(sent_lens), up_w, down_w)
        return (hidden.astype(jnp.float32) + mixed).astype(jnp.bfloat16)
    middles = lax.map(forward_section, (section_ids, hidden_fwd, routes_fwd, probs_fwd, norm_gains, w_in, w_out))
    memory = middles[first_decoder - 1]
    src_fwd = lengths[0].reshape(N_EXPERT, SENTS)
    src_bwd = lengths[2].reshape(N_EXPERT, SENTS)
    attend_all = jax.vmap(cross_attend, in_axes=(0, 0, 0, None, None, None, None))

    def attend_section(items):
        section, middle, gains, query_w, keyval_w, output_w = items
        attended = attend_all(blocks(middle), blocks(memory), src_fwd, gains[1], query_w, keyval_w, output_w).reshape(ROWS, D)
        return jnp.where(section >= first_decoder, attended, middle)
    outputs = lax.map(attend_section, (section_ids, middles, norm_gains, w_query, w_keyval, w_output))
    passed_rows = jnp.roll(outputs, 1, axis=0)
    memory_blocks = blocks(memory_saved)

    def backward_section(carry, items):
        section, hidden, middle, cotangent, routes, probs, gains, up_w, down_w, query_w, keyval_w, output_w = items
        is_decoder = section >= first_decoder

        def attend(mid_rows, mem_rows):
            return attend_all(mid_rows, mem_rows, src_bwd, gains[1], query_w, keyval_w, output_w)
        _, attend_grad = jax.vjp(attend, blocks(middle), memory_blocks)
        grad_mid, grad_memory = attend_grad(blocks(cotangent))
        upstream = jnp.where(is_decoder, grad_mid.reshape(ROWS, D), cotangent)
        memory_term = jnp.where(is_decoder, grad_memory.reshape(ROWS, D).astype(jnp.float32), 0.0)
        sent_lens = jnp.where(is_decoder, lengths[3], lengths[2])
        normed = layer_norm(hidden, gains[0]).astype(jnp.bfloat16)
        grad_units = expert_grad(normed, routes, probs, live_rows(sent_lens), upstream.astype(jnp.float32), up_w, down_w)

        def norm_only(inputs):
            return layer_norm(inputs, gains[0])
        _, norm_grad = jax.vjp(norm_only, hidden.astype(jnp.float32))
        grad_hidden = (upstream.astype(jnp.float32) + norm_grad(grad_units)[0]).astype(jnp.bfloat16)
        return (carry + memory_term, grad_hidden)
    memory_total, grad_rows = lax.scan(backward_section, jnp.zeros((ROWS, D), jnp.float32), (section_ids, hidden_bwd, mid_bwd, grads_in, routes_bwd, probs_bwd, norm_gains, w_in, w_out, w_query, w_keyval, w_output))
    passed_grads = jnp.roll(grad_rows, -1, axis=0)
    memory_grad = memory_total.astype(jnp.bfloat16)
    return (passed_rows, passed_grads, memory_grad)
```

```python
import functools

import jax
import jax.numpy as jnp
from jax import lax
from jax.experimental import pallas as pl
from jax.experimental.pallas import tpu as pltpu
from jax.sharding import PartitionSpec as P

MESH = pl.DeviceIdType.MESH
HEAD_DIM = 64
EXPERTS = 4
SEQ = 32
NZ = 8
NY = 4
NSEC = 16
TOK = 64
LINE = NY * TOK
D = 1024
HALF = LINE // 2

EPS = 1e-05
ROOT_HALF = 0.7071067811865476
INV_ROOT_TWO_PI = 0.3989422804014327


def layer_norm(row_block, gain_row):
    values = row_block.astype(jnp.float32)
    center = values - jnp.mean(values, axis=-1, keepdims=True)
    spread = jnp.mean(center * center, axis=-1, keepdims=True)
    return center * lax.rsqrt(spread + EPS) * gain_row


def gelu_value(inputs):
    return 0.5 * inputs * (1.0 + lax.erf(inputs * ROOT_HALF))


def gelu_slope(inputs):
    return (
        0.5 * (1.0 + lax.erf(inputs * ROOT_HALF))
        + inputs * jnp.exp(-0.5 * inputs * inputs) * INV_ROOT_TWO_PI
    )


def row_lengths(sent_lens, row_count):
    sentence = jnp.arange(row_count) // SEQ
    sent_match = sentence[:, None] == jnp.arange(sent_lens.shape[0])[None, :]
    return jnp.sum(jnp.where(sent_match, sent_lens[None, :], 0), axis=1)


def cross_attend(middle, memory, src_len, gain_row, query_w, keyval_w, output_w):
    row_count = middle.shape[0]
    inner_width = query_w.shape[1]
    head_count = inner_width // HEAD_DIM
    normed = layer_norm(middle, gain_row).astype(jnp.bfloat16)
    query_rows = jnp.dot(normed, query_w, preferred_element_type=jnp.float32).astype(jnp.bfloat16)
    keyval = jnp.dot(memory, keyval_w, preferred_element_type=jnp.float32).astype(jnp.bfloat16)
    q_heads = query_rows.reshape(row_count, head_count, HEAD_DIM).astype(jnp.float32)
    k_heads = keyval[:, :inner_width].reshape(row_count, head_count, HEAD_DIM).astype(jnp.float32)
    v_heads = keyval[:, inner_width:].reshape(row_count, head_count, HEAD_DIM).astype(jnp.float32)
    scores = jnp.einsum("qhd,khd->hqk", q_heads, k_heads) * HEAD_DIM ** (-0.5)
    row_index = jnp.arange(row_count)
    sentence = row_index // SEQ
    key_len = row_lengths(src_len, row_count)
    allowed = (sentence[:, None] == sentence[None, :]) & (
        (row_index % SEQ)[None, :] < key_len[None, :]
    )
    raised = jnp.where(allowed[None], jnp.exp(scores), 0.0)
    weights = (raised / jnp.sum(raised, axis=-1, keepdims=True)).astype(jnp.bfloat16)
    mixed_heads = jnp.einsum("hqk,khd->qhd", weights.astype(jnp.float32), v_heads).astype(
        jnp.bfloat16
    )
    projected = jnp.dot(
        mixed_heads.reshape(row_count, inner_width), output_w, preferred_element_type=jnp.float32
    )
    return (middle.astype(jnp.float32) + projected).astype(jnp.bfloat16)


def place():
    me = lax.axis_index("expert")
    return me, lax.div(me, NY), lax.rem(me, NY)


def to_expert(z, y):
    return {"expert": lax.rem(z + 2 * NZ, NZ) * NY + lax.rem(y + 2 * NY, NY)}


def to_section(s):
    return {"section": lax.rem(s + 2 * NSEC, NSEC)}


def rows(ref, start, count):
    return ref.at[pl.ds(pl.multiple_of(start, 8), count)]


def remote(src, dst, send, recv, device):
    return pltpu.make_async_remote_copy(
        src_ref=src, dst_ref=dst, send_sem=send, recv_sem=recv, device_id=device, device_id_type=MESH
    )


def greet(devices):
    barrier = pltpu.get_barrier_semaphore()
    for device in devices:
        pl.semaphore_signal(barrier, inc=1, device_id=device, device_id_type=MESH)
    pl.semaphore_wait(barrier, len(devices))


def expert_neighbours():
    _, z, y = place()
    return [to_expert(z + 1, y), to_expert(z - 1, y)] + [to_expert(z, y + d) for d in (1, 2, 3)]


class Gather:
    def __init__(self, src, dst, local, ysend, yrecv, zsend, zrecv):
        self.src, self.dst, self.local = src, dst, local
        self.ysend, self.yrecv, self.zsend, self.zrecv = ysend, yrecv, zsend, zrecv
        self.size = src.shape[0]
        self.me, self.z, self.y = place()

    def own(self):
        return pltpu.make_async_copy(
            self.src, rows(self.dst, self.me * self.size, self.size), self.local
        )

    def line(self, d, arriving):
        index = self.z * NY + lax.rem(self.y + NY - d, NY) if arriving else self.me
        block = rows(self.dst, index * self.size, self.size)
        return remote(
            self.src, block, self.ysend.at[d - 1], self.yrecv.at[d - 1], to_expert(self.z, self.y + d)
        )

    def hop(self, way, step, arriving):
        sign = 1 if way == 0 else -1
        back = step + 1 if arriving else step
        origin = lax.rem(self.z - sign * back + 2 * NZ, NZ)
        start, count = origin * NY * self.size, NY * self.size
        if step == 3:
            count = count // 2
            start = start + way * count
        block = rows(self.dst, start, count)
        return remote(
            block, block, self.zsend.at[way, step], self.zrecv.at[way, step], to_expert(self.z + sign, self.y)
        )

    def begin(self):
        self.own().start()
        for d in (1, 2, 3):
            self.line(d, False).start()

    def step(self, s):
        if s == 0:
            self.own().wait()
            for d in (1, 2, 3):
                self.line(d, True).wait_recv()
        else:
            for way in (0, 1):
                self.hop(way, s - 1, True).wait_recv()
        for way in (0, 1):
            if s < 4:
                self.hop(way, s, False).start()

    def finish(self):
        for d in (1, 2, 3):
            self.line(d, False).wait_send()
        for way in (0, 1):
            for s in range(4):
                self.hop(way, s, False).wait_send()


GATHER_SEMS = [
    pltpu.SemaphoreType.DMA,
    pltpu.SemaphoreType.DMA((3,)),
    pltpu.SemaphoreType.DMA((3,)),
    pltpu.SemaphoreType.DMA((2, 4)),
    pltpu.SemaphoreType.DMA((2, 4)),
]


class Scatter:
    def __init__(self, src, slots, line_buf, line_slots, zsend, zrecv, ysend, yrecv):
        self.src, self.slots, self.line_buf, self.line_slots = src, slots, line_buf, line_slots
        self.zsend, self.zrecv, self.ysend, self.yrecv = zsend, zrecv, ysend, yrecv
        self.me, self.z, self.y = place()

    def mine(self, way, step, chunk):
        sign = 1 if way == 0 else -1
        dest = lax.rem(self.z + sign * (4 - step) + 2 * NZ, NZ)
        return pl.ds(pl.multiple_of(dest * LINE + chunk * HALF, HALF), HALF)

    def hop(self, way, step, chunk):
        sign = 1 if way == 0 else -1
        part = pl.ds(chunk * HALF, HALF)
        first = 0 if chunk == way else 1
        if step == first:
            source = self.src.at[self.mine(way, step, chunk)]
        else:
            source = self.slots.at[way, step - 1, part]
        return remote(
            source,
            self.slots.at[way, step, part],
            self.zsend.at[way, step, chunk],
            self.zrecv.at[way, step, chunk],
            to_expert(self.z + sign, self.y),
        )

    def step(self, s):
        for chunk in (0, 1):
            for way in (0, 1):
                first = 0 if chunk == way else 1
                part = pl.ds(chunk * HALF, HALF)
                if s < first:
                    continue
                if s > first:
                    self.hop(way, s - 1, chunk).wait_recv()
                    if s < 4:
                        self.slots[way, s - 1, part] = (
                            self.slots[way, s - 1, part].astype(jnp.float32)
                            + self.src[self.mine(way, s, chunk)].astype(jnp.float32)
                        ).astype(jnp.bfloat16)
                if s < 4:
                    self.hop(way, s, chunk).start()

    def line(self, d):
        target = lax.rem(self.y + d, NY)
        return remote(
            rows(self.line_buf, target * TOK, TOK),
            self.line_slots.at[d - 1],
            self.ysend.at[d - 1],
            self.yrecv.at[d - 1],
            to_expert(self.z, self.y + d),
        )

    def cross(self):
        for chunk in (0, 1):
            part = pl.ds(chunk * HALF, HALF)
            own = self.src[pl.ds(pl.multiple_of(self.z * LINE + chunk * HALF, HALF), HALF)]
            self.line_buf[part] = (
                own.astype(jnp.float32)
                + self.slots[0, 3, part].astype(jnp.float32)
                + self.slots[1, 3, part].astype(jnp.float32)
            ).astype(jnp.bfloat16)
        for d in (1, 2, 3):
            self.line(d).start()

    def total(self):
        for d in (1, 2, 3):
            self.line(d).wait_recv()
        result = self.line_buf[pl.ds(pl.multiple_of(self.y * TOK, TOK), TOK)].astype(jnp.float32)
        for d in (1, 2, 3):
            result = result + self.line_slots[d - 1].astype(jnp.float32)
        return result

    def finish(self):
        for chunk in (0, 1):
            for way in (0, 1):
                for s in range(0 if chunk == way else 1, 4):
                    self.hop(way, s, chunk).wait_send()
        for d in (1, 2, 3):
            self.line(d).wait_send()


SCATTER_SCRATCH = [
    pltpu.VMEM((2, 4, LINE, D), jnp.bfloat16),
    pltpu.VMEM((LINE, D), jnp.bfloat16),
    pltpu.VMEM((3, TOK, D), jnp.bfloat16),
    pltpu.SemaphoreType.DMA((2, 4, 2)),
    pltpu.SemaphoreType.DMA((2, 4, 2)),
    pltpu.SemaphoreType.DMA((3,)),
    pltpu.SemaphoreType.DMA((3,)),
]


def gather_kernel(count, *refs):
    srcs, dsts, sems = refs[:count], refs[count : 2 * count], refs[2 * count :]
    gathers = [Gather(srcs[i], dsts[i], *sems[5 * i : 5 * i + 5]) for i in range(count)]
    greet(expert_neighbours())
    for g in gathers:
        g.begin()
    for s in range(5):
        for g in gathers:
            g.step(s)
    for g in gathers:
        g.finish()


def all_gathered(arrays):
    count = len(arrays)
    return pl.pallas_call(
        functools.partial(gather_kernel, count),
        out_shape=[
            jax.ShapeDtypeStruct((NZ * NY * a.shape[0],) + a.shape[1:], a.dtype) for a in arrays
        ],
        in_specs=[pl.BlockSpec(memory_space=pl.ANY)] * count,
        out_specs=[pl.BlockSpec(memory_space=pl.ANY)] * count,
        scratch_shapes=GATHER_SEMS * count,
        compiler_params=pltpu.CompilerParams(
            collective_id=0, has_side_effects=True, vmem_limit_bytes=48 * 2**20
        ),
        name="gather_rows_weights",
    )(*arrays)


def scatter_gather_kernel(part_ref, grad_ref, total_ref, gathered_ref, *scratch):
    scatter = Scatter(part_ref, *scratch[:7])
    gather = Gather(grad_ref, gathered_ref, *scratch[7:])
    greet(expert_neighbours())
    gather.begin()
    for s in range(5):
        scatter.step(s)
        gather.step(s)
    scatter.cross()
    total_ref[...] = scatter.total()
    gather.finish()
    scatter.finish()


def scatter_and_gather(partial_rows, grad_rows):
    return pl.pallas_call(
        scatter_gather_kernel,
        out_shape=[
            jax.ShapeDtypeStruct((TOK, D), jnp.float32),
            jax.ShapeDtypeStruct((NZ * NY * TOK, D), jnp.bfloat16),
        ],
        in_specs=[pl.BlockSpec(memory_space=pltpu.VMEM), pl.BlockSpec(memory_space=pl.ANY)],
        out_specs=[pl.BlockSpec(memory_space=pltpu.VMEM), pl.BlockSpec(memory_space=pl.ANY)],
        scratch_shapes=SCATTER_SCRATCH + GATHER_SEMS,
        compiler_params=pltpu.CompilerParams(
            collective_id=1, has_side_effects=True, vmem_limit_bytes=48 * 2**20
        ),
        name="scatter_outputs_gather_grads",
    )(partial_rows, grad_rows)


PIECE_ROWS = 32
PIECE_COLS = 128


def piece(ref, index):
    row = pl.multiple_of(lax.div(index, 8) * PIECE_ROWS, PIECE_ROWS)
    col = pl.multiple_of(lax.rem(index, 8) * PIECE_COLS, PIECE_COLS)
    return ref.at[pl.ds(row, PIECE_ROWS), pl.ds(col, PIECE_COLS)]


def scatter_section_kernel(root, *refs):
    (part_ref, mid_ref, term_ref, total_ref, memory_ref, grad_ref, mem_buf, terms, grad_buf) = refs[:9]
    (bsend, brecv, tsend, trecv, gsend, grecv) = refs[9:15]
    scatter = Scatter(part_ref, *refs[15:])
    s = lax.axis_index("section")
    greet(expert_neighbours() + [to_section(s + d) for d in range(1, NSEC)])

    def spread(slot, target):
        return remote(mem_buf, mem_buf, bsend.at[slot], brecv, to_section(target))

    is_root = s == root
    is_leader = lax.rem(s, 4) == root % 4

    @pl.when(is_root)
    def _():
        mem_buf[...] = mid_ref[...]
        for slot in (0, 1, 2):
            spread(slot, s + 4 * (slot + 1)).start()

    def term(d):
        target = lax.rem(s + d, NSEC)
        return remote(piece(term_ref, target), terms.at[d - 1], tsend.at[d - 1], trecv.at[d - 1], to_section(s + d))

    for d in range(1, NSEC):
        term(d).start()
    scatter.step(0)
    scatter.step(1)

    @pl.when(jnp.logical_not(is_root))
    def _():
        spread(0, s + 1).wait_recv()

    @pl.when(is_leader)
    def _():
        for slot, d in ((3, 1), (4, -1), (5, -2)):
            spread(slot, s + d).start()

    for d in range(1, NSEC):
        term(d).wait_recv()
    own = piece(term_ref, s)[...].astype(jnp.float32)
    for d in range(1, NSEC):
        own = own + terms[d - 1].astype(jnp.float32)
    own_view = piece(grad_buf, s)
    own_view[...] = own.astype(jnp.bfloat16)

    def result(d, arriving):
        index = lax.rem(s + NSEC - d, NSEC) if arriving else s
        view = piece(grad_buf, index)
        return remote(view, view, gsend.at[d - 1], grecv.at[d - 1], to_section(s + d))

    for d in range(1, NSEC):
        result(d, False).start()
    scatter.step(2)
    scatter.step(3)
    scatter.step(4)
    scatter.cross()
    for d in range(1, NSEC):
        result(d, True).wait_recv()
    grad_ref[...] = grad_buf[...]
    memory_ref[...] = mem_buf[...]
    total_ref[...] = scatter.total()
    for d in range(1, NSEC):
        term(d).wait_send()
        result(d, False).wait_send()

    @pl.when(is_root)
    def _():
        for slot in (0, 1, 2):
            spread(slot, s + 4).wait_send()

    @pl.when(is_leader)
    def _():
        for slot in (3, 4, 5):
            spread(slot, s + 1).wait_send()

    scatter.finish()


def scatter_and_sections(root, partial_rows, middle, memory_term):
    return pl.pallas_call(
        functools.partial(scatter_section_kernel, root),
        out_shape=[
            jax.ShapeDtypeStruct((TOK, D), jnp.float32),
            jax.ShapeDtypeStruct((TOK, D), jnp.bfloat16),
            jax.ShapeDtypeStruct((TOK, D), jnp.bfloat16),
        ],
        in_specs=[pl.BlockSpec(memory_space=pltpu.VMEM)] * 3,
        out_specs=[pl.BlockSpec(memory_space=pltpu.VMEM)] * 3,
        scratch_shapes=[
            pltpu.VMEM((TOK, D), jnp.bfloat16),
            pltpu.VMEM((NSEC - 1, PIECE_ROWS, PIECE_COLS), jnp.bfloat16),
            pltpu.VMEM((TOK, D), jnp.bfloat16),
            pltpu.SemaphoreType.DMA((6,)),
            pltpu.SemaphoreType.DMA,
            pltpu.SemaphoreType.DMA((NSEC - 1,)),
            pltpu.SemaphoreType.DMA((NSEC - 1,)),
            pltpu.SemaphoreType.DMA((NSEC - 1,)),
            pltpu.SemaphoreType.DMA((NSEC - 1,)),
        ]
        + SCATTER_SCRATCH,
        compiler_params=pltpu.CompilerParams(
            collective_id=2, has_side_effects=True, vmem_limit_bytes=48 * 2**20
        ),
        name="scatter_grads_spread_memory",
    )(partial_rows, middle, memory_term)


def pass_kernel(rows_ref, grads_ref, rows_out, grads_out, rows_slot, grads_slot, send, recv):
    s = lax.axis_index("section")
    ahead, behind = to_section(s + 1), to_section(s - 1)
    greet([ahead, behind])
    forward = remote(rows_ref, rows_slot, send.at[0], recv.at[0], ahead)
    backward = remote(grads_ref, grads_slot, send.at[1], recv.at[1], behind)
    forward.start()
    backward.start()
    forward.wait_recv()
    rows_out[...] = rows_slot[...]
    backward.wait_recv()
    grads_out[...] = grads_slot[...]
    forward.wait_send()
    backward.wait_send()


def passed(out_rows, grad_rows):
    shape = jax.ShapeDtypeStruct((TOK, D), jnp.bfloat16)
    return pl.pallas_call(
        pass_kernel,
        out_shape=[shape, shape],
        in_specs=[pl.BlockSpec(memory_space=pltpu.VMEM)] * 2,
        out_specs=[pl.BlockSpec(memory_space=pltpu.VMEM)] * 2,
        scratch_shapes=[
            pltpu.VMEM((TOK, D), jnp.bfloat16),
            pltpu.VMEM((TOK, D), jnp.bfloat16),
            pltpu.SemaphoreType.DMA((2,)),
            pltpu.SemaphoreType.DMA((2,)),
        ],
        compiler_params=pltpu.CompilerParams(collective_id=3, has_side_effects=True),
        name="pass_rows_grads",
    )(out_rows, grad_rows)


def expert_shares(routes, probs, live):
    named = routes[:, :, None] == jnp.arange(EXPERTS)[None, None, :]
    return jnp.sum(jnp.where(named, probs[:, :, None], 0.0), axis=1) * live[:, None]


def on_device(
    hidden_fwd,
    hidden_bwd,
    mid_bwd,
    grads_in,
    memory_saved,
    lengths,
    routes_fwd,
    routes_bwd,
    probs_fwd,
    probs_bwd,
    norm_gains,
    w_in,
    w_out,
    w_query,
    w_keyval,
    w_output,
):
    first_decoder = 3
    is_decoder = lax.axis_index("section") >= first_decoder
    my_expert = lax.axis_index("expert") // 8
    gain_moe = norm_gains[0, 0]
    gain_att = norm_gains[0, 1]
    up_slice = w_in[0]
    down_slice = w_out[0]
    position = jnp.arange(TOK) % SEQ
    lens_fwd = jnp.where(is_decoder, lengths[1], lengths[0])
    lens_bwd = jnp.where(is_decoder, lengths[3], lengths[2])
    live_fwd = (position < row_lengths(lens_fwd, TOK)).astype(jnp.float32)
    live_bwd = (position < row_lengths(lens_bwd, TOK)).astype(jnp.float32)
    hidden_a = hidden_fwd[0]
    hidden_b = hidden_bwd[0]
    normed_a = layer_norm(hidden_a, gain_moe).astype(jnp.bfloat16)
    normed_b = layer_norm(hidden_b, gain_moe).astype(jnp.bfloat16)
    shares = jnp.concatenate(
        [
            expert_shares(routes_fwd[0], probs_fwd[0], live_fwd).T,
            expert_shares(routes_bwd[0], probs_bwd[0], live_bwd).T,
        ],
        axis=1,
    )
    shares = jnp.concatenate([shares, jnp.zeros_like(shares)], axis=0)
    all_a, all_b, keyval_w, query_w, output_w, all_shares = all_gathered(
        [normed_a, normed_b, w_keyval[0], w_query[0], w_output[0], shares]
    )
    all_shares = lax.dynamic_index_in_dim(
        all_shares.reshape(NZ * NY, 8, 2 * TOK), my_expert, axis=1, keepdims=False
    )
    share_a = all_shares[:, :TOK].reshape(-1, 1)
    share_b = all_shares[:, TOK:].reshape(-1, 1)
    cotangent = grads_in[0]

    def attend_saved(mid_rows, mem_rows):
        return cross_attend(mid_rows, mem_rows, lengths[2], gain_att, query_w, keyval_w, output_w)

    _, attend_grad = jax.vjp(attend_saved, mid_bwd[0], memory_saved)
    grad_mid, grad_memory = attend_grad(cotangent)
    upstream = jnp.where(is_decoder, grad_mid, cotangent)
    memory_term = jnp.where(is_decoder, grad_memory, jnp.zeros_like(grad_memory))

    units = gelu_value(jnp.dot(all_a, up_slice, preferred_element_type=jnp.float32)).astype(
        jnp.bfloat16
    )
    part_a = (jnp.dot(units, down_slice, preferred_element_type=jnp.float32) * share_a).astype(
        jnp.bfloat16
    )
    mixed_a, all_grads = scatter_and_gather(part_a, upstream)
    middle_a = (hidden_a.astype(jnp.float32) + mixed_a).astype(jnp.bfloat16)

    sent_rows = (all_grads.astype(jnp.float32) * share_b).astype(jnp.bfloat16)
    pre_act = jnp.dot(all_b, up_slice, preferred_element_type=jnp.float32)
    through = lax.dot_general(
        sent_rows, down_slice, (((1,), (1,)), ((), ())), preferred_element_type=jnp.float32
    )
    unit_grad = (through * gelu_slope(pre_act)).astype(jnp.bfloat16)
    part_b = lax.dot_general(
        unit_grad, up_slice, (((1,), (1,)), ((), ())), preferred_element_type=jnp.float32
    ).astype(jnp.bfloat16)
    grad_units, memory, memory_grad = scatter_and_sections(
        first_decoder - 1, part_b, middle_a, memory_term
    )
    attended = cross_attend(middle_a, memory, lengths[0], gain_att, query_w, keyval_w, output_w)
    out_a = jnp.where(is_decoder, attended, middle_a)

    def norm_only(inputs):
        return layer_norm(inputs, gain_moe)

    _, norm_grad = jax.vjp(norm_only, hidden_b.astype(jnp.float32))
    grad_hidden = (upstream.astype(jnp.float32) + norm_grad(grad_units)[0]).astype(jnp.bfloat16)
    passed_rows, passed_grads = passed(out_a, grad_hidden)
    return (passed_rows[None], passed_grads[None], memory_grad)


def solution(mesh):
    return jax.shard_map(
        on_device,
        mesh=mesh,
        in_specs=(
            P("section", "expert", None),
            P("section", "expert", None),
            P("section", "expert", None),
            P("section", "expert", None),
            P("expert", None),
            P(None, "expert"),
            P("section", "expert", None),
            P("section", "expert", None),
            P("section", "expert", None),
            P("section", "expert", None),
            P("section", None, None),
            P("section", None, "expert"),
            P("section", "expert", None),
            P("section", "expert", None),
            P("section", "expert", None),
            P("section", "expert", None),
        ),
        out_specs=(P("section", "expert", None), P("section", "expert", None), P("expert", None)),
        check_vma=False,
    )
```

```python
import functools

import jax
import jax.numpy as jnp
from jax import lax
from jax.experimental import pallas as pl
from jax.experimental.pallas import tpu as pltpu
from jax.sharding import PartitionSpec as P

MESH = pl.DeviceIdType.MESH
BF16 = jnp.bfloat16
F32 = jnp.float32
HEAD_DIM = 64
EXPERTS = 4
SEQ = 32
NZ = 8
NY = 4
NSEC = 16
FIRST_DECODER = 3
ROOT = FIRST_DECODER - 1
TOK = 64
LINE = NY * TOK
HALF = LINE // 2
ROWS = NZ * LINE
D = 1024
UNITS = 512
INNER = 512
PAIR = 2 * HEAD_DIM

EPS = 1e-05
ROOT_HALF = 0.7071067811865476
INV_ROOT_TWO_PI = 0.3989422804014327


def dot_nn(a, b):
    return lax.dot_general(a, b, (((1,), (0,)), ((), ())), preferred_element_type=F32)


def dot_nt(a, b):
    return lax.dot_general(a, b, (((1,), (1,)), ((), ())), preferred_element_type=F32)


def dot_tn(a, b):
    return lax.dot_general(a, b, (((0,), (0,)), ((), ())), preferred_element_type=F32)


def norm_parts(row_block):
    values = row_block.astype(F32)
    center = values - jnp.mean(values, axis=-1, keepdims=True)
    spread = jnp.mean(center * center, axis=-1, keepdims=True)
    scale = lax.rsqrt(spread + EPS)
    return center * scale, scale


def norm_rows(row_block, gain_row):
    return (norm_parts(row_block)[0] * gain_row).astype(BF16)


def norm_grad(row_block, gain_row, upstream):
    unit, scale = norm_parts(row_block)
    grad = upstream * gain_row
    mean_grad = jnp.mean(grad, axis=-1, keepdims=True)
    mean_along = jnp.mean(grad * unit, axis=-1, keepdims=True)
    return scale * (grad - mean_grad - unit * mean_along)


def gelu_value(inputs):
    return 0.5 * inputs * (1.0 + lax.erf(inputs * ROOT_HALF))


def gelu_slope(inputs):
    return (
        0.5 * (1.0 + lax.erf(inputs * ROOT_HALF))
        + inputs * jnp.exp(-0.5 * inputs * inputs) * INV_ROOT_TWO_PI
    )


def allowed_keys(len_first, len_second):
    row = lax.broadcasted_iota(jnp.int32, (TOK, TOK), 0)
    col = lax.broadcasted_iota(jnp.int32, (TOK, TOK), 1)
    col_len = jnp.where(col < SEQ, len_first, len_second)
    same = (row < SEQ) == (col < SEQ)
    return same & (jnp.where(col < SEQ, col, col - SEQ) < col_len)


def live_column(len_first, len_second):
    row = lax.broadcasted_iota(jnp.int32, (TOK, 1), 0)
    row_len = jnp.where(row < SEQ, len_first, len_second)
    return jnp.where(jnp.where(row < SEQ, row, row - SEQ) < row_len, 1.0, 0.0)


def one_head(values, side):
    lane = lax.broadcasted_iota(jnp.int32, values.shape, 1)
    return jnp.where((lane < HEAD_DIM) == (side == 0), values, jnp.zeros_like(values))


def head_weights(query, key, allowed):
    scores = dot_nt(query, key) * HEAD_DIM ** (-0.5)
    raised = jnp.where(allowed, jnp.exp(scores), 0.0)
    return raised / jnp.sum(raised, axis=-1, keepdims=True)


def mix_pair(query, key, value, allowed):
    mixed = jnp.zeros((TOK, PAIR), F32)
    for side in (0, 1):
        weights = head_weights(one_head(query, side), key, allowed).astype(BF16)
        mixed = mixed + dot_nn(weights, one_head(value, side))
    return mixed.astype(BF16)


def mix_pair_grad(query, key, value, d_mixed, allowed):
    d_query = jnp.zeros((TOK, PAIR), F32)
    d_key = jnp.zeros((TOK, PAIR), F32)
    d_value = jnp.zeros((TOK, PAIR), F32)
    for side in (0, 1):
        query_one, grad_one = one_head(query, side), one_head(d_mixed, side)
        exact = head_weights(query_one, key, allowed)
        d_weights = dot_nt(grad_one, value).astype(BF16).astype(F32)
        d_value = d_value + dot_tn(exact.astype(BF16), grad_one)
        along = jnp.sum(d_weights * exact, axis=-1, keepdims=True)
        d_scores = (exact * (d_weights - along) * HEAD_DIM ** (-0.5)).astype(BF16)
        d_query = d_query + dot_nn(d_scores, one_head(key, side))
        d_key = d_key + dot_tn(d_scores, query_one)
    return d_query.astype(BF16), d_key.astype(BF16), d_value.astype(BF16)


def turned(column):
    eye = lax.broadcasted_iota(jnp.int32, (TOK, TOK), 0) == lax.broadcasted_iota(
        jnp.int32, (TOK, TOK), 1
    )
    return jnp.sum(jnp.where(eye, column, 0.0), axis=0, keepdims=True)


def upright(row):
    eye = lax.broadcasted_iota(jnp.int32, (TOK, TOK), 0) == lax.broadcasted_iota(
        jnp.int32, (TOK, TOK), 1
    )
    return jnp.sum(jnp.where(eye, row, 0.0), axis=1, keepdims=True)


def place():
    me = lax.axis_index("expert")
    return me, lax.div(me, NY), lax.rem(me, NY)


def to_expert(z, y):
    return {"expert": lax.rem(z + 2 * NZ, NZ) * NY + lax.rem(y + 2 * NY, NY)}


def to_section(s):
    return {"section": lax.rem(s + 2 * NSEC, NSEC)}


def remote(src, dst, send, recv, device):
    return pltpu.make_async_remote_copy(
        src_ref=src, dst_ref=dst, send_sem=send, recv_sem=recv, device_id=device, device_id_type=MESH
    )


class Gather:
    def __init__(self, array, size, first_col, cols, ysend, yrecv, zsend, zrecv):
        self.array, self.size, self.cols = array, size, pl.ds(first_col, cols)
        self.ysend, self.yrecv, self.zsend, self.zrecv = ysend, yrecv, zsend, zrecv
        self.me, self.z, self.y = place()

    def block(self, start, count):
        return self.array.at[pl.ds(pl.multiple_of(start, 8), count), self.cols]

    def line(self, d, arriving):
        index = self.z * NY + lax.rem(self.y + NY - d, NY) if arriving else self.me
        block = self.block(index * self.size, self.size)
        return remote(
            block, block, self.ysend.at[d - 1], self.yrecv.at[d - 1], to_expert(self.z, self.y + d)
        )

    def hop(self, way, step, arriving):
        sign = 1 if way == 0 else -1
        back = step + 1 if arriving else step
        origin = lax.rem(self.z - sign * back + 2 * NZ, NZ)
        start, count = origin * NY * self.size, NY * self.size
        if step == 3:
            count = count // 2
            start = start + way * count
        block = self.block(start, count)
        return remote(
            block,
            block,
            self.zsend.at[way, step],
            self.zrecv.at[way, step],
            to_expert(self.z + sign, self.y),
        )

    def begin(self):
        for d in (1, 2, 3):
            self.line(d, False).start()

    def step(self, s):
        if s == 0:
            for d in (1, 2, 3):
                self.line(d, True).wait_recv()
        for way in (0, 1):
            if s > 0:
                self.hop(way, s - 1, True).wait_recv()
            if s < 4:
                self.hop(way, s, False).start()

    def finish(self):
        for d in (1, 2, 3):
            self.line(d, False).wait_send()
        for way in (0, 1):
            for s in range(4):
                self.hop(way, s, False).wait_send()


GATHER_SEMS = [
    pltpu.SemaphoreType.DMA((3,)),
    pltpu.SemaphoreType.DMA((3,)),
    pltpu.SemaphoreType.DMA((2, 4)),
    pltpu.SemaphoreType.DMA((2, 4)),
]


class Scatter:
    def __init__(self, src, slots, line_buf, line_slots, zsend, zrecv, ysend, yrecv):
        self.src, self.slots, self.line_buf, self.line_slots = src, slots, line_buf, line_slots
        self.zsend, self.zrecv, self.ysend, self.yrecv = zsend, zrecv, ysend, yrecv
        self.me, self.z, self.y = place()

    def mine(self, way, step, chunk):
        sign = 1 if way == 0 else -1
        dest = lax.rem(self.z + sign * (4 - step) + 2 * NZ, NZ)
        return pl.ds(pl.multiple_of(dest * LINE + chunk * HALF, HALF), HALF)

    def hop(self, way, step, chunk):
        sign = 1 if way == 0 else -1
        part = pl.ds(chunk * HALF, HALF)
        first = 0 if chunk == way else 1
        if step == first:
            source = self.src.at[self.mine(way, step, chunk)]
        else:
            source = self.slots.at[way, step - 1, part]
        return remote(
            source,
            self.slots.at[way, step, part],
            self.zsend.at[way, step, chunk],
            self.zrecv.at[way, step, chunk],
            to_expert(self.z + sign, self.y),
        )

    def step(self, s):
        for chunk in (0, 1):
            for way in (0, 1):
                first = 0 if chunk == way else 1
                part = pl.ds(chunk * HALF, HALF)
                if s < first:
                    continue
                if s > first:
                    self.hop(way, s - 1, chunk).wait_recv()
                    if s < 4:
                        self.slots[way, s - 1, part] = (
                            self.slots[way, s - 1, part].astype(F32)
                            + self.src[self.mine(way, s, chunk)].astype(F32)
                        ).astype(BF16)
                if s < 4:
                    self.hop(way, s, chunk).start()

    def line(self, d):
        target = lax.rem(self.y + d, NY)
        return remote(
            self.line_buf.at[pl.ds(pl.multiple_of(target * TOK, TOK), TOK)],
            self.line_slots.at[d - 1],
            self.ysend.at[d - 1],
            self.yrecv.at[d - 1],
            to_expert(self.z, self.y + d),
        )

    def cross(self):
        for chunk in (0, 1):
            part = pl.ds(chunk * HALF, HALF)
            own = self.src[pl.ds(pl.multiple_of(self.z * LINE + chunk * HALF, HALF), HALF)]
            self.line_buf[part] = (
                own.astype(F32)
                + self.slots[0, 3, part].astype(F32)
                + self.slots[1, 3, part].astype(F32)
            ).astype(BF16)
        for d in (1, 2, 3):
            self.line(d).start()

    def total(self):
        for d in (1, 2, 3):
            self.line(d).wait_recv()
        result = self.line_buf[pl.ds(pl.multiple_of(self.y * TOK, TOK), TOK)].astype(F32)
        for d in (1, 2, 3):
            result = result + self.line_slots[d - 1].astype(F32)
        return result

    def finish(self):
        for chunk in (0, 1):
            for way in (0, 1):
                for s in range(0 if chunk == way else 1, 4):
                    self.hop(way, s, chunk).wait_send()
        for d in (1, 2, 3):
            self.line(d).wait_send()


SCATTER_SCRATCH = [
    pltpu.VMEM((2, 4, LINE, D), BF16),
    pltpu.VMEM((LINE, D), BF16),
    pltpu.VMEM((3, TOK, D), BF16),
    pltpu.SemaphoreType.DMA((2, 4, 2)),
    pltpu.SemaphoreType.DMA((2, 4, 2)),
    pltpu.SemaphoreType.DMA((3,)),
    pltpu.SemaphoreType.DMA((3,)),
]

PIECE_ROWS = 32
PIECE_COLS = 128


def piece(ref, index):
    row = pl.multiple_of(lax.div(index, 8) * PIECE_ROWS, PIECE_ROWS)
    col = pl.multiple_of(lax.rem(index, 8) * PIECE_COLS, PIECE_COLS)
    return ref.at[pl.ds(row, PIECE_ROWS), pl.ds(col, PIECE_COLS)]


class Sections:
    def __init__(self, memory, term_rows, terms, total, bsend, brecv, tsend, trecv, gsend, grecv, psend, precv):
        self.memory, self.term_rows, self.terms, self.sum_rows = memory, term_rows, terms, total
        self.bsend, self.brecv, self.tsend, self.trecv = bsend, brecv, tsend, trecv
        self.gsend, self.grecv, self.psend, self.precv = gsend, grecv, psend, precv
        self.s = lax.axis_index("section")
        self.is_root = self.s == ROOT
        self.is_leader = lax.rem(self.s, 4) == ROOT % 4

    def spread(self, slot, d):
        return remote(self.memory, self.memory, self.bsend.at[slot], self.brecv, to_section(self.s + d))

    def spread_root(self, middle):
        @pl.when(self.is_root)
        def _():
            self.memory[...] = middle[...]
            for slot in (0, 1, 2):
                self.spread(slot, 4 * (slot + 1)).start()

    def spread_leader(self):
        @pl.when(self.is_leader & jnp.logical_not(self.is_root))
        def _():
            self.spread(0, 4).wait_recv()

        @pl.when(self.is_leader)
        def _():
            for slot, d in ((3, -2), (4, -1), (5, 1)):
                self.spread(slot, d).start()

    def spread_wait(self):
        @pl.when(jnp.logical_not(self.is_leader))
        def _():
            self.spread(0, 4).wait_recv()

    def spread_finish(self):
        @pl.when(self.is_root)
        def _():
            for slot in (0, 1, 2):
                self.spread(slot, 4).wait_send()

        @pl.when(self.is_leader)
        def _():
            for slot in (3, 4, 5):
                self.spread(slot, 1).wait_send()

    def term(self, d):
        target = lax.rem(self.s + d, NSEC)
        return remote(
            piece(self.term_rows, target),
            self.terms.at[d - 1],
            self.tsend.at[d - 1],
            self.trecv.at[d - 1],
            to_section(self.s + d),
        )

    def terms_begin(self):
        for d in range(1, NSEC):
            self.term(d).start()

    def result(self, d, arriving):
        index = lax.rem(self.s + NSEC - d, NSEC) if arriving else self.s
        view = piece(self.sum_rows, index)
        return remote(view, view, self.gsend.at[d - 1], self.grecv.at[d - 1], to_section(self.s + d))

    def terms_sum(self):
        own = piece(self.term_rows, self.s)[...].astype(F32)
        for d in range(1, NSEC):
            self.term(d).wait_recv()
            own = own + self.terms[d - 1].astype(F32)
        view = piece(self.sum_rows, self.s)
        view[...] = own.astype(BF16)
        for d in range(1, NSEC):
            self.result(d, False).start()

    def terms_finish(self):
        for d in range(1, NSEC):
            self.result(d, True).wait_recv()
        for d in range(1, NSEC):
            self.term(d).wait_send()
            self.result(d, False).wait_send()

    def passing(self, src, dst, d, slot):
        return remote(src, dst, self.psend.at[slot], self.precv.at[slot], to_section(self.s + d))


def kernel(
    hidden_a, hidden_b, mid_b, cotangent, mem_saved, lengths,
    routes_f, routes_b, probs_f, probs_b, gains, w_in, w_out, w_query, w_keyval, w_output,
    rows_out, grads_out, memory_grad_out,
    all_query, all_keyval, all_output, all_shares, all_a, all_x, all_d, part_a, part_b,
    query, key, value, mixed, middle, upstream, out_rows, grad_rows,
    memory, term_rows, terms, *sems
):
    sems = list(sems)

    def take(count):
        taken = sems[:count]
        del sems[:count]
        return taken

    me, z, y = place()
    my_expert = lax.div(me, NZ)
    section = lax.axis_index("section")
    is_decoder = section >= FIRST_DECODER
    gain_moe = gains[0:1, :]
    gain_att = gains[1:2, :]

    g_wo = Gather(all_output, 16, 0, D, *take(4))
    g_wq = Gather(all_query, 32, 0, INNER, *take(4))
    g_wkv = Gather(all_keyval, 32, 0, D, *take(4))
    g_sh = Gather(all_shares, 8, 0, 128, *take(4))
    g_a = [Gather(all_a, TOK, c * 512, 512, *take(4)) for c in (0, 1)]
    g_x = [Gather(all_x, TOK, c * 512, 512, *take(4)) for c in (0, 1)]
    g_d = [Gather(all_d, TOK, c * 512, 512, *take(4)) for c in (0, 1)]
    scatter_a = Scatter(part_a, *take(7))
    scatter_b = Scatter(part_b, *take(7))
    sections = Sections(memory, term_rows, terms, memory_grad_out, *take(8))

    partners = (
        [to_expert(z + 1, y), to_expert(z - 1, y)]
        + [to_expert(z, y + d) for d in (1, 2, 3)]
        + [to_section(section + d) for d in range(1, NSEC)]
    )
    barrier = pltpu.get_barrier_semaphore()
    for device in partners:
        pl.semaphore_signal(barrier, inc=1, device_id=device, device_id_type=MESH)

    def own_rows(ref, size):
        return ref.at[pl.ds(pl.multiple_of(me * size, size), size)]

    own_rows(all_output, 16)[...] = w_output[...]
    own_rows(all_query, 32)[...] = w_query[...]
    own_rows(all_keyval, 32)[...] = w_keyval[...]
    own_rows(all_a, TOK)[...] = norm_rows(hidden_a[...], gain_moe)
    own_rows(all_x, TOK)[...] = norm_rows(hidden_b[...], gain_moe)
    own_shares = own_rows(all_shares, 8)
    own_shares[...] = jnp.zeros((8, 128), F32)
    for base, routes, probs, line in ((0, routes_f, probs_f, 0), (4, routes_b, probs_b, 2)):
        live = live_column(
            jnp.where(is_decoder, lengths[line + 1, 0], lengths[line, 0]),
            jnp.where(is_decoder, lengths[line + 1, 1], lengths[line, 1]),
        )
        for e in range(EXPERTS):
            share = jnp.where(routes[:, 0:1] == e, probs[:, 0:1], 0.0) + jnp.where(
                routes[:, 1:2] == e, probs[:, 1:2], 0.0
            )
            own_shares[base + e : base + e + 1, 0:TOK] = turned(share * live)
    pl.semaphore_wait(barrier, len(partners))

    def share_column(block, i, base):
        row = all_shares[pl.ds((block * NY + i) * 8 + base + my_expert, 1), 0:TOK]
        return upright(row)

    def line_rows(block):
        return pl.ds(pl.multiple_of(block * LINE, LINE), LINE)

    def expert_forward(block, _):
        units = gelu_value(dot_nn(all_a[line_rows(block)], w_in[...])).astype(BF16)
        part = dot_nn(units, w_out[...])
        for i in range(NY):
            part_a[pl.ds(pl.multiple_of(block * LINE + i * TOK, TOK), TOK)] = (
                part[i * TOK : (i + 1) * TOK] * share_column(block, i, 0)
            ).astype(BF16)
        return 0

    def expert_backward(block, _):
        for i in range(NY):
            part = pl.ds(pl.multiple_of(block * LINE + i * TOK, TOK), TOK)
            all_d_row = all_d[part].astype(F32) * share_column(block, i, 4)
            part_b[part] = all_d_row.astype(BF16)
        through = dot_nt(part_b[line_rows(block)], w_out[...])
        slope = gelu_slope(dot_nn(all_x[line_rows(block)], w_in[...]))
        unit_grad = (through * slope).astype(BF16)
        part_b[line_rows(block)] = dot_nt(unit_grad, w_in[...]).astype(BF16)
        return 0

    def project(mid_rows, mem_rows):
        query[...] = dot_nn(norm_rows(mid_rows, gain_att), all_query[...]).astype(BF16)
        key[...] = dot_nn(mem_rows, all_keyval[:, :INNER]).astype(BF16)
        value[...] = dot_nn(mem_rows, all_keyval[:, INNER:]).astype(BF16)

    def mix_grads(pairs):
        allowed = allowed_keys(lengths[2, 0], lengths[2, 1])
        for p in pairs:
            at = slice(p * PAIR, (p + 1) * PAIR)
            grads = mix_pair_grad(query[:, at], key[:, at], value[:, at], mixed[:, at], allowed)
            query[:, at], key[:, at], value[:, at] = grads

    def attend_grads():
        d_normed = dot_nt(query[...], all_query[...]).astype(BF16).astype(F32)
        d_memory = dot_nt(key[...], all_keyval[:, :INNER]) + dot_nt(value[...], all_keyval[:, INNER:])
        term_rows[...] = jnp.where(is_decoder, d_memory, 0.0).astype(BF16)
        through = norm_grad(mid_b[...], gain_att, d_normed).astype(BF16).astype(F32)
        cot = cotangent[...].astype(F32)
        upstream[...] = jnp.where(is_decoder, cot + through, cot).astype(BF16)
        own_rows(all_d, TOK)[...] = upstream[...]

    weights, side_a = [g_wo, g_wq, g_wkv], [g_sh] + g_a
    for g in weights + side_a + g_x:
        g.begin()
    for s in range(4):
        for g in weights:
            g.step(s)
    for g in side_a:
        g.step(0)
    for g in weights:
        g.step(4)

    for s in range(1, 4):
        for g in side_a:
            g.step(s)
        if s == 1:
            project(mid_b[...], mem_saved[...])
            mixed[...] = dot_nt(cotangent[...], all_output[...]).astype(BF16)
        else:
            mix_grads((0, 1) if s == 2 else (2, 3))
    for g in g_x:
        g.step(0)
    attend_grads()
    for g in g_d:
        g.begin()
    sections.terms_begin()
    for g in side_a:
        g.step(4)

    for s in range(1, 4):
        for g in g_x:
            g.step(s)
        lax.fori_loop(2 * s - 2, 2 * s, expert_forward, 0)
    for g in g_d:
        g.step(0)
    for g in g_x:
        g.step(4)
    lax.fori_loop(6, 8, expert_forward, 0)

    g_d[0].step(1)
    g_d[1].step(1)
    sections.terms_sum()
    for s in range(2, 4):
        for g in g_d:
            g.step(s)
    scatter_a.step(0)
    for g in g_d:
        g.step(4)

    lax.fori_loop(0, 2, expert_backward, 0)
    scatter_a.step(1)
    lax.fori_loop(2, 4, expert_backward, 0)
    scatter_a.step(2)
    lax.fori_loop(4, 6, expert_backward, 0)
    scatter_a.step(3)
    lax.fori_loop(6, 8, expert_backward, 0)
    scatter_b.step(0)
    scatter_a.step(4)
    scatter_a.cross()

    scatter_b.step(1)
    middle[...] = (hidden_a[...].astype(F32) + scatter_a.total()).astype(BF16)
    sections.spread_root(middle)
    sections.spread_leader()
    scatter_b.step(2)
    sections.spread_wait()
    project(middle[...], memory[...])
    allowed = allowed_keys(lengths[0, 0], lengths[0, 1])
    for p in range(INNER // PAIR):
        at = slice(p * PAIR, (p + 1) * PAIR)
        mixed[:, at] = mix_pair(query[:, at], key[:, at], value[:, at], allowed)
    scatter_b.step(3)
    projected = jnp.where(is_decoder, dot_nn(mixed[...], all_output[...]), 0.0)
    out_rows[...] = (middle[...].astype(F32) + projected).astype(BF16)
    ahead = sections.passing(out_rows, rows_out, 1, 0)
    ahead.start()
    scatter_b.step(4)
    scatter_b.cross()
    sections.terms_finish()
    for g in weights + side_a + g_x + g_d:
        g.finish()
    scatter_a.finish()
    sections.spread_finish()
    through = norm_grad(hidden_b[...], gain_moe, scatter_b.total())
    grad_rows[...] = (upstream[...].astype(F32) + through).astype(BF16)
    behind = sections.passing(grad_rows, grads_out, -1, 1)
    behind.start()
    scatter_b.finish()
    ahead.wait()
    behind.wait()


def on_device(
    hidden_fwd,
    hidden_bwd,
    mid_bwd,
    grads_in,
    memory_saved,
    lengths,
    routes_fwd,
    routes_bwd,
    probs_fwd,
    probs_bwd,
    norm_gains,
    w_in,
    w_out,
    w_query,
    w_keyval,
    w_output,
):
    shape = jax.ShapeDtypeStruct((TOK, D), BF16)
    vmem = pl.BlockSpec(memory_space=pltpu.VMEM)
    smem = pl.BlockSpec(memory_space=pltpu.SMEM)
    row_buf = pltpu.VMEM((ROWS, D), BF16)
    tok_buf = pltpu.VMEM((TOK, D), BF16)
    inner_buf = pltpu.VMEM((TOK, INNER), BF16)
    passed_rows, passed_grads, memory_grad = pl.pallas_call(
        kernel,
        out_shape=[shape] * 3,
        in_specs=[vmem] * 5 + [smem] + [vmem] * 10,
        out_specs=[vmem] * 3,
        scratch_shapes=[
            pltpu.VMEM((D, INNER), BF16),
            pltpu.VMEM((D, 2 * INNER), BF16),
            pltpu.VMEM((INNER, D), BF16),
            pltpu.VMEM((NZ * NY * 8, 128), F32),
            row_buf,
            row_buf,
            row_buf,
            row_buf,
            row_buf,
            inner_buf,
            inner_buf,
            inner_buf,
            inner_buf,
            tok_buf,
            tok_buf,
            tok_buf,
            tok_buf,
            tok_buf,
            tok_buf,
            pltpu.VMEM((NSEC - 1, PIECE_ROWS, PIECE_COLS), BF16),
        ]
        + GATHER_SEMS * 10
        + SCATTER_SCRATCH * 2
        + [
            pltpu.SemaphoreType.DMA((6,)),
            pltpu.SemaphoreType.DMA,
            pltpu.SemaphoreType.DMA((NSEC - 1,)),
            pltpu.SemaphoreType.DMA((NSEC - 1,)),
            pltpu.SemaphoreType.DMA((NSEC - 1,)),
            pltpu.SemaphoreType.DMA((NSEC - 1,)),
            pltpu.SemaphoreType.DMA((2,)),
            pltpu.SemaphoreType.DMA((2,)),
        ],
        compiler_params=pltpu.CompilerParams(
            collective_id=0, has_side_effects=True, vmem_limit_bytes=56 * 2**20
        ),
        name="relay_step",
    )(
        hidden_fwd[0],
        hidden_bwd[0],
        mid_bwd[0],
        grads_in[0],
        memory_saved,
        lengths,
        routes_fwd[0],
        routes_bwd[0],
        probs_fwd[0],
        probs_bwd[0],
        norm_gains[0],
        w_in[0],
        w_out[0],
        w_query[0],
        w_keyval[0],
        w_output[0],
    )
    return (passed_rows[None], passed_grads[None], memory_grad)


def solution(mesh):
    return jax.shard_map(
        on_device,
        mesh=mesh,
        in_specs=(
            P("section", "expert", None),
            P("section", "expert", None),
            P("section", "expert", None),
            P("section", "expert", None),
            P("expert", None),
            P(None, "expert"),
            P("section", "expert", None),
            P("section", "expert", None),
            P("section", "expert", None),
            P("section", "expert", None),
            P("section", None, None),
            P("section", None, "expert"),
            P("section", "expert", None),
            P("section", "expert", None),
            P("section", "expert", None),
            P("section", "expert", None),
        ),
        out_specs=(P("section", "expert", None), P("section", "expert", None), P("expert", None)),
        check_vma=False,
    )
```

```python
import functools

import jax
import jax.numpy as jnp
from jax import lax
from jax.experimental import pallas as pl
from jax.experimental.pallas import tpu as pltpu
from jax.sharding import PartitionSpec as P

MESH = pl.DeviceIdType.MESH
BF16 = jnp.bfloat16
F32 = jnp.float32
HEAD_DIM = 64
EXPERTS = 4
SEQ = 32
NZ = 8
NY = 4
NSEC = 16
FIRST_DECODER = 3
ROOT = FIRST_DECODER - 1
TOK = 64
LINE = NY * TOK
D = 1024
CUT_A, CUT_X, CUT_D, CUT_RA, CUT_RB = 768, 896, 768, 768, 896
UNITS = 512
INNER = 512
PAIR = 2 * HEAD_DIM

EPS = 1e-05
ROOT_HALF = 0.7071067811865476
INV_ROOT_TWO_PI = 0.3989422804014327


def dot_nn(a, b):
    return lax.dot_general(a, b, (((1,), (0,)), ((), ())), preferred_element_type=F32)


def dot_nt(a, b):
    return lax.dot_general(a, b, (((1,), (1,)), ((), ())), preferred_element_type=F32)


def dot_tn(a, b):
    return lax.dot_general(a, b, (((0,), (0,)), ((), ())), preferred_element_type=F32)


def norm_parts(row_block):
    values = row_block.astype(F32)
    center = values - jnp.mean(values, axis=-1, keepdims=True)
    spread = jnp.mean(center * center, axis=-1, keepdims=True)
    scale = lax.rsqrt(spread + EPS)
    return center * scale, scale


def norm_rows(row_block, gain_row):
    return (norm_parts(row_block)[0] * gain_row).astype(BF16)


def norm_grad(row_block, gain_row, upstream):
    unit, scale = norm_parts(row_block)
    grad = upstream * gain_row
    mean_grad = jnp.mean(grad, axis=-1, keepdims=True)
    mean_along = jnp.mean(grad * unit, axis=-1, keepdims=True)
    return scale * (grad - mean_grad - unit * mean_along)


def gelu_value(inputs):
    return 0.5 * inputs * (1.0 + lax.erf(inputs * ROOT_HALF))


def gelu_slope(inputs):
    return (
        0.5 * (1.0 + lax.erf(inputs * ROOT_HALF))
        + inputs * jnp.exp(-0.5 * inputs * inputs) * INV_ROOT_TWO_PI
    )


def allowed_keys(len_first, len_second):
    row = lax.broadcasted_iota(jnp.int32, (TOK, TOK), 0)
    col = lax.broadcasted_iota(jnp.int32, (TOK, TOK), 1)
    col_len = jnp.where(col < SEQ, len_first, len_second)
    same = (row < SEQ) == (col < SEQ)
    return same & (jnp.where(col < SEQ, col, col - SEQ) < col_len)


def live_row(len_first, len_second):
    col = lax.broadcasted_iota(jnp.int32, (1, TOK), 1)
    col_len = jnp.where(col < SEQ, len_first, len_second)
    return jnp.where(jnp.where(col < SEQ, col, col - SEQ) < col_len, 1.0, 0.0)


def one_head(values, side):
    lane = lax.broadcasted_iota(jnp.int32, values.shape, 1)
    return jnp.where((lane < HEAD_DIM) == (side == 0), values, jnp.zeros_like(values))


def head_weights(query, key, allowed):
    scores = dot_nt(query, key) * HEAD_DIM ** (-0.5)
    raised = jnp.where(allowed, jnp.exp(scores), 0.0)
    return raised / jnp.sum(raised, axis=-1, keepdims=True)


def mix_pair(query, key, value, allowed):
    mixed = jnp.zeros((TOK, PAIR), F32)
    for side in (0, 1):
        weights = head_weights(one_head(query, side), key, allowed).astype(BF16)
        mixed = mixed + dot_nn(weights, one_head(value, side))
    return mixed.astype(BF16)


def mix_pair_grad(query, key, value, d_mixed, allowed):
    d_query = jnp.zeros((TOK, PAIR), F32)
    d_key = jnp.zeros((TOK, PAIR), F32)
    d_value = jnp.zeros((TOK, PAIR), F32)
    for side in (0, 1):
        query_one, grad_one = one_head(query, side), one_head(d_mixed, side)
        exact = head_weights(query_one, key, allowed)
        d_weights = dot_nt(grad_one, value).astype(BF16).astype(F32)
        d_value = d_value + dot_tn(exact.astype(BF16), grad_one)
        along = jnp.sum(d_weights * exact, axis=-1, keepdims=True)
        d_scores = (exact * (d_weights - along) * HEAD_DIM ** (-0.5)).astype(BF16)
        d_query = d_query + dot_nn(d_scores, one_head(key, side))
        d_key = d_key + dot_tn(d_scores, query_one)
    return d_query.astype(BF16), d_key.astype(BF16), d_value.astype(BF16)


def upright(row):
    eye = lax.broadcasted_iota(jnp.int32, (TOK, TOK), 0) == lax.broadcasted_iota(
        jnp.int32, (TOK, TOK), 1
    )
    return jnp.sum(jnp.where(eye, row, 0.0), axis=1, keepdims=True)


def place():
    me = lax.axis_index("expert")
    return me, lax.div(me, NY), lax.rem(me, NY)


def to_expert(z, y):
    return {"expert": lax.rem(z + 2 * NZ, NZ) * NY + lax.rem(y + 2 * NY, NY)}


def to_section(s):
    return {"section": lax.rem(s + 2 * NSEC, NSEC)}


def remote(src, dst, send, recv, device):
    return pltpu.make_async_remote_copy(
        src_ref=src, dst_ref=dst, send_sem=send, recv_sem=recv, device_id=device, device_id_type=MESH
    )


class Ring:
    def __init__(self, view, send, recv):
        self.view, self.send, self.recv = view, send, recv
        _, self.z, self.y = place()

    def hop(self, way, step, arriving):
        sign = 1 if way == 0 else -1
        back = step + 1 if arriving else step
        origin = lax.rem(self.z - sign * back + 2 * NZ, NZ)
        block = self.view(origin, way if step == 3 else None)
        return remote(
            block, block, self.send.at[way, step], self.recv.at[way, step], to_expert(self.z + sign, self.y)
        )

    def step(self, s):
        for way in (0, 1):
            if s > 0:
                self.hop(way, s - 1, True).wait_recv()
            if s < 4:
                self.hop(way, s, False).start()

    def finish(self):
        for way in (0, 1):
            for s in range(4):
                self.hop(way, s, False).wait_send()


class Line:
    def __init__(self, view, send, recv):
        self.view, self.send, self.recv = view, send, recv
        _, self.z, self.y = place()

    def copy(self, d, arriving):
        block = self.view(lax.rem(self.y + NY - d, NY) if arriving else self.y)
        return remote(block, block, self.send.at[d - 1], self.recv.at[d - 1], to_expert(self.z, self.y + d))

    def begin(self):
        for d in (1, 2, 3):
            self.copy(d, False).start()

    def arrive(self):
        for d in (1, 2, 3):
            self.copy(d, True).wait_recv()

    def finish(self):
        for d in (1, 2, 3):
            self.copy(d, False).wait_send()


def halves(cut):
    first = (cut // 128 + 1) // 2 * 128
    return (0, first), (first, cut - first)


class Gather:
    def __init__(self, array, first_col, cols, ysend, yrecv, zsend, zrecv):
        _, z, _ = place()
        at = pl.ds(first_col, cols)
        self.line = Line(lambda y: array.at[z, y, :, at], ysend, yrecv)

        def view(origin, half):
            if half is None:
                return array.at[origin, :, :, at]
            return array.at[origin, pl.ds(half * 2, 2), :, at]

        self.ring = Ring(view, zsend, zrecv)

    def begin(self):
        self.line.begin()

    def step(self, s):
        if s == 0:
            self.line.arrive()
        self.ring.step(s)

    def finish(self):
        self.line.finish()
        self.ring.finish()


class CrossGather:
    def __init__(self, array, first_col, cols, ysend, yrecv, zsend, zrecv):
        _, _, me_y = place()
        at = pl.ds(first_col, cols)
        rows = array.shape[2] // 2

        def view(origin, half):
            if half is None:
                return array.at[origin, me_y, :, at]
            return array.at[origin, me_y, pl.ds(half * rows, rows), at]

        self.ring = Ring(view, zsend, zrecv)
        self.line = Line(lambda y: array.at[:, y, :, at], ysend, yrecv)

    def step(self, s):
        self.ring.step(s)

    def begin_line(self):
        self.line.begin()

    def arrive(self):
        self.line.arrive()

    def finish(self):
        self.ring.finish()
        self.line.finish()


GATHER_SEMS = [
    pltpu.SemaphoreType.DMA((3,)),
    pltpu.SemaphoreType.DMA((3,)),
    pltpu.SemaphoreType.DMA((2, 4)),
    pltpu.SemaphoreType.DMA((2, 4)),
]


class SumRing:
    def __init__(self, own, slot, send, recv):
        self.own, self.slot, self.send, self.recv = own, slot, send, recv
        _, self.z, self.y = place()

    def term(self, way, step, chunk):
        sign = 1 if way == 0 else -1
        return self.own(lax.rem(self.z + sign * (4 - step) + 2 * NZ, NZ), chunk)

    def hop(self, way, step, chunk):
        first = 0 if chunk == way else 1
        source = self.term(way, step, chunk) if step == first else self.slot(way, step - 1, chunk)
        return remote(
            source,
            self.slot(way, step, chunk),
            self.send.at[way, step, chunk],
            self.recv.at[way, step, chunk],
            to_expert(self.z + (1 if way == 0 else -1), self.y),
        )

    def step(self, s, chunks=(0, 1)):
        for chunk in chunks:
            for way in (0, 1):
                first = 0 if chunk == way else 1
                if s < first:
                    continue
                if s > first:
                    self.hop(way, s - 1, chunk).wait_recv()
                    if s < 4:
                        slot = self.slot(way, s - 1, chunk)
                        slot[...] = (
                            slot[...].astype(F32) + self.term(way, s, chunk)[...].astype(F32)
                        ).astype(BF16)
                if s < 4:
                    self.hop(way, s, chunk).start()

    def total(self, chunk):
        return (
            self.own(self.z, chunk)[...].astype(F32)
            + self.slot(0, 3, chunk)[...].astype(F32)
            + self.slot(1, 3, chunk)[...].astype(F32)
        )

    def finish(self):
        for chunk in (0, 1):
            for way in (0, 1):
                for s in range(0 if chunk == way else 1, 4):
                    self.hop(way, s, chunk).wait_send()


class SumLine:
    def __init__(self, src, slot, send, recv):
        self.src, self.slot, self.send, self.recv = src, slot, send, recv
        _, self.z, self.y = place()

    def copy(self, d, chunk):
        return remote(
            self.src(lax.rem(self.y + d, NY), chunk),
            self.slot(d, chunk),
            self.send.at[chunk, d - 1],
            self.recv.at[chunk, d - 1],
            to_expert(self.z, self.y + d),
        )

    def begin(self, chunk):
        for d in (1, 2, 3):
            self.copy(d, chunk).start()

    def arrive(self):
        for chunk in (0, 1):
            for d in (1, 2, 3):
                self.copy(d, chunk).wait_recv()

    def finish(self):
        for chunk in (0, 1):
            for d in (1, 2, 3):
                self.copy(d, chunk).wait_send()


class DirectSum:
    def __init__(self, src, slots, send, recv):
        self.src, self.slots, self.send, self.recv = src, slots, send, recv
        _, self.z, self.y = place()

    def copy(self, d):
        return remote(
            self.src(lax.rem(self.y + d, NY)),
            self.slots.at[d - 1],
            self.send.at[d - 1],
            self.recv.at[d - 1],
            to_expert(self.z, self.y + d),
        )

    def begin(self):
        for d in (1, 2, 3):
            self.copy(d).start()

    def total(self, sums):
        for d in (1, 2, 3):
            self.copy(d).wait_recv()
        own = self.src(self.y)

        def add(block, _):
            result = own[block].astype(F32)
            for d in (1, 2, 3):
                result = result + self.slots[d - 1, block].astype(F32)
            sums[block] = result.astype(BF16)
            return 0

        lax.fori_loop(0, NZ, add, 0)

    def finish(self):
        for d in (1, 2, 3):
            self.copy(d).wait_send()


class Scatter:
    def __init__(self, cut, src, slots, line_buf, line_slots, zsend, zrecv, ysend, yrecv):
        def part(chunk):
            return pl.ds(*halves(cut)[chunk])

        self.part, self.line_buf, self.line_slots = part, line_buf, line_slots
        self.ring = SumRing(
            lambda dest, chunk: src.at[dest, :, :, part(chunk)],
            lambda way, step, chunk: slots.at[way, step, :, :, part(chunk)],
            zsend,
            zrecv,
        )
        self.line = SumLine(
            lambda y, chunk: line_buf.at[y, :, part(chunk)],
            lambda d, chunk: line_slots.at[d - 1, :, part(chunk)],
            ysend,
            yrecv,
        )

    def step(self, s):
        self.ring.step(s)

    def cross(self):
        for chunk in (0, 1):
            self.ring.step(4, (chunk,))
            self.line_buf[:, :, self.part(chunk)] = self.ring.total(chunk).astype(BF16)
            self.line.begin(chunk)

    def total(self):
        self.line.arrive()
        result = self.line_buf[self.line.y].astype(F32)
        for d in (1, 2, 3):
            result = result + self.line_slots[d - 1].astype(F32)
        return result

    def finish(self):
        self.ring.finish()
        self.line.finish()


class CrossScatter:
    def __init__(self, cut, src, line_slots, sums, slots, ysend, yrecv, zsend, zrecv):
        at = pl.ds(cut, D - cut)
        self.sums = sums
        self.line = DirectSum(lambda y: src.at[:, y, :, at], line_slots, ysend, yrecv)
        self.ring = SumRing(
            lambda dest, chunk: sums.at[dest, pl.ds(chunk * 32, 32)],
            lambda way, step, chunk: slots.at[way, step, pl.ds(chunk * 32, 32)],
            zsend,
            zrecv,
        )

    def begin(self):
        self.line.begin()

    def sum_line(self):
        self.line.total(self.sums)

    def step(self, s):
        self.ring.step(s)

    def total(self):
        return jnp.concatenate([self.ring.total(0), self.ring.total(1)], axis=0)

    def finish(self):
        self.line.finish()
        self.ring.finish()


def scatter_scratch(cut):
    return [
        pltpu.VMEM((2, 4, NY, TOK, cut), BF16),
        pltpu.VMEM((NY, TOK, cut), BF16),
        pltpu.VMEM((3, TOK, cut), BF16),
    ] + [pltpu.SemaphoreType.DMA(dims) for dims in ((2, 4, 2), (2, 4, 2), (2, 3), (2, 3))]


def cross_scratch(cut):
    return [
        pltpu.VMEM((3, NZ, TOK, D - cut), BF16),
        pltpu.VMEM((NZ, TOK, D - cut), BF16),
        pltpu.VMEM((2, 4, TOK, D - cut), BF16),
    ] + [pltpu.SemaphoreType.DMA(dims) for dims in ((3,), (3,), (2, 4, 2), (2, 4, 2))]


PIECE_ROWS = 32
PIECE_COLS = 128


def piece(ref, index):
    row = pl.multiple_of(lax.div(index, 8) * PIECE_ROWS, PIECE_ROWS)
    col = pl.multiple_of(lax.rem(index, 8) * PIECE_COLS, PIECE_COLS)
    return ref.at[pl.ds(row, PIECE_ROWS), pl.ds(col, PIECE_COLS)]


class Sections:
    def __init__(self, memory, term_rows, terms, total, bsend, brecv, tsend, trecv, gsend, grecv, psend, precv):
        self.memory, self.term_rows, self.terms, self.sum_rows = memory, term_rows, terms, total
        self.bsend, self.brecv, self.tsend, self.trecv = bsend, brecv, tsend, trecv
        self.gsend, self.grecv, self.psend, self.precv = gsend, grecv, psend, precv
        self.s = lax.axis_index("section")
        self.is_root = self.s == ROOT
        self.is_leader = lax.rem(self.s, 4) == ROOT % 4

    def spread(self, slot, d):
        return remote(self.memory, self.memory, self.bsend.at[slot], self.brecv, to_section(self.s + d))

    def spread_root(self, middle):
        @pl.when(self.is_root)
        def _():
            self.memory[...] = middle[...]
            for slot in (0, 1, 2):
                self.spread(slot, 4 * (slot + 1)).start()

    def spread_leader(self):
        @pl.when(self.is_leader & jnp.logical_not(self.is_root))
        def _():
            self.spread(0, 4).wait_recv()

        @pl.when(self.is_leader)
        def _():
            for slot, d in ((3, -2), (4, -1), (5, 1)):
                self.spread(slot, d).start()

    def spread_wait(self):
        @pl.when(jnp.logical_not(self.is_leader))
        def _():
            self.spread(0, 4).wait_recv()

    def spread_finish(self):
        @pl.when(self.is_root)
        def _():
            for slot in (0, 1, 2):
                self.spread(slot, 4).wait_send()

        @pl.when(self.is_leader)
        def _():
            for slot in (3, 4, 5):
                self.spread(slot, 1).wait_send()

    def term(self, d):
        target = lax.rem(self.s + d, NSEC)
        return remote(
            piece(self.term_rows, target),
            self.terms.at[d - 1],
            self.tsend.at[d - 1],
            self.trecv.at[d - 1],
            to_section(self.s + d),
        )

    def terms_begin(self):
        for d in range(1, NSEC):
            self.term(d).start()

    def result(self, d, arriving):
        index = lax.rem(self.s + NSEC - d, NSEC) if arriving else self.s
        view = piece(self.sum_rows, index)
        return remote(view, view, self.gsend.at[d - 1], self.grecv.at[d - 1], to_section(self.s + d))

    def terms_sum(self):
        own = piece(self.term_rows, self.s)[...].astype(F32)
        for d in range(1, NSEC):
            self.term(d).wait_recv()
            own = own + self.terms[d - 1].astype(F32)
        view = piece(self.sum_rows, self.s)
        view[...] = own.astype(BF16)
        for d in range(1, NSEC):
            self.result(d, False).start()

    def terms_finish(self):
        for d in range(1, NSEC):
            self.result(d, True).wait_recv()
        for d in range(1, NSEC):
            self.term(d).wait_send()
            self.result(d, False).wait_send()

    def passing(self, src, dst, d, slot):
        return remote(src, dst, self.psend.at[slot], self.precv.at[slot], to_section(self.s + d))


def kernel(
    hidden_a, hidden_b, mid_b, cotangent, mem_saved, lengths,
    routes_f, routes_b, probs_f, probs_b, gains, w_in, w_out, w_query, w_keyval, w_output,
    rows_out, grads_out, memory_grad_out,
    all_query, all_keyval, all_output, all_shares, all_a, all_x, all_d, part_a, part_b, slopes,
    query, key, value, mixed, middle, upstream, out_rows, grad_rows,
    memory, term_rows, terms, *sems
):
    sems = list(sems)

    def take(count):
        taken = sems[:count]
        del sems[:count]
        return taken

    me, z, y = place()
    my_expert = lax.div(me, NZ)
    section = lax.axis_index("section")
    is_decoder = section >= FIRST_DECODER
    gain_moe = gains[0:1, :]
    gain_att = gains[1:2, :]

    g_wo = Gather(all_output, 0, D, *take(4))
    g_wkv = [Gather(all_keyval, c * INNER, INNER, *take(4)) for c in (0, 1)]
    g_sh = Gather(all_shares, 0, 128, *take(4))
    g_a = [Gather(all_a, *at, *take(4)) for at in halves(CUT_A)]
    g_x = [Gather(all_x, *at, *take(4)) for at in halves(CUT_X)]
    g_d = [Gather(all_d, *at, *take(4)) for at in halves(CUT_D)]
    c_wq = CrossGather(all_query, 0, INNER, *take(4))
    c_a = CrossGather(all_a, CUT_A, D - CUT_A, *take(4))
    c_x = CrossGather(all_x, CUT_X, D - CUT_X, *take(4))
    c_d = CrossGather(all_d, CUT_D, D - CUT_D, *take(4))
    scatter_a = Scatter(CUT_RA, part_a, *take(7))
    scatter_b = Scatter(CUT_RB, part_b, *take(7))
    cross_a = CrossScatter(CUT_RA, part_a, *take(7))
    cross_b = CrossScatter(CUT_RB, part_b, *take(7))
    sections = Sections(memory, term_rows, terms, memory_grad_out, *take(8))

    partners = (
        [to_expert(z + 1, y), to_expert(z - 1, y)]
        + [to_expert(z, y + d) for d in (1, 2, 3)]
        + [to_section(section + d) for d in range(1, NSEC)]
    )
    barrier = pltpu.get_barrier_semaphore()
    for device in partners:
        pl.semaphore_signal(barrier, inc=1, device_id=device, device_id_type=MESH)

    all_output[z, y] = w_output[...]
    all_query[z, y] = w_query[...]
    all_keyval[z, y] = w_keyval[...]
    all_a[z, y] = norm_rows(hidden_a[...], gain_moe)
    all_x[z, y] = norm_rows(hidden_b[...], gain_moe)
    own_shares = all_shares.at[z, y]
    own_shares[...] = jnp.zeros((8, 128), F32)
    for base, routes, probs, line in ((0, routes_f, probs_f, 0), (4, routes_b, probs_b, 2)):
        live = live_row(
            jnp.where(is_decoder, lengths[0, line + 1], lengths[0, line]),
            jnp.where(is_decoder, lengths[1, line + 1], lengths[1, line]),
        )
        for e in range(EXPERTS):
            share = jnp.where(routes[0:1, :] == e, probs[0:1, :], 0.0) + jnp.where(
                routes[1:2, :] == e, probs[1:2, :], 0.0
            )
            own_shares[base + e : base + e + 1, 0:TOK] = share * live
    pl.semaphore_wait(barrier, len(partners))

    def share_column(block, i, base):
        return upright(all_shares[block, i, pl.ds(base + my_expert, 1), 0:TOK])

    def line_rows(ref, block):
        return ref[block].reshape(LINE, D)

    def expert_forward(block, _):
        units = gelu_value(dot_nn(line_rows(all_a, block), w_in[...])).astype(BF16)
        part = dot_nn(units, w_out[...])
        for i in range(NY):
            share = share_column(block, i, 0)
            part_a[block, i] = (part[i * TOK : (i + 1) * TOK] * share).astype(BF16)
        return 0

    def expert_slopes(block, _):
        slopes[block] = gelu_slope(dot_nn(line_rows(all_x, block), w_in[...]))
        return 0

    def expert_backward(block, _):
        for i in range(NY):
            part_b[block, i] = (all_d[block, i].astype(F32) * share_column(block, i, 4)).astype(BF16)
        unit_grad = (dot_nt(line_rows(part_b, block), w_out[...]) * slopes[block]).astype(BF16)
        part_b[block] = dot_nt(unit_grad, w_in[...]).astype(BF16).reshape(NY, TOK, D)
        return 0

    def query_weights():
        return all_query[...].reshape(D, INNER)

    def keyval_weights(first):
        return all_keyval[:, :, :, first : first + INNER].reshape(D, INNER)

    def output_weights():
        return all_output[...].reshape(INNER, D)

    def project_memory(mem_rows):
        key[...] = dot_nn(mem_rows, keyval_weights(0)).astype(BF16)
        value[...] = dot_nn(mem_rows, keyval_weights(INNER)).astype(BF16)

    def project_query(mid_rows):
        query[...] = dot_nn(norm_rows(mid_rows, gain_att), query_weights()).astype(BF16)

    def mix_grads(pairs):
        allowed = allowed_keys(lengths[0, 2], lengths[1, 2])
        for p in pairs:
            at = slice(p * PAIR, (p + 1) * PAIR)
            grads = mix_pair_grad(query[:, at], key[:, at], value[:, at], mixed[:, at], allowed)
            query[:, at], key[:, at], value[:, at] = grads

    def attend_grads():
        d_normed = dot_nt(query[...], query_weights()).astype(BF16).astype(F32)
        d_memory = dot_nt(key[...], keyval_weights(0)) + dot_nt(value[...], keyval_weights(INNER))
        term_rows[...] = jnp.where(is_decoder, d_memory, 0.0).astype(BF16)
        through = norm_grad(mid_b[...], gain_att, d_normed).astype(BF16).astype(F32)
        cot = cotangent[...].astype(F32)
        upstream[...] = jnp.where(is_decoder, cot + through, cot).astype(BF16)
        all_d[z, y] = upstream[...]

    weights, side_a = [g_wo] + g_wkv, [g_sh] + g_a
    crosses = [c_wq, c_a, c_x]

    for g in weights + side_a:
        g.begin()
    for s in range(5):
        for c in crosses:
            c.step(s)
        if s < 3:
            weights[s].step(0)
    for g in weights:
        g.step(1)
    c_wq.begin_line()
    for g in weights:
        g.step(2)
    for g in g_x:
        g.begin()
    c_a.begin_line()
    for g in weights:
        g.step(3)
    for g in side_a:
        g.step(0)
    for g in weights:
        g.step(4)

    for g in side_a:
        g.step(1)
    project_memory(mem_saved[...])
    mixed[...] = dot_nt(cotangent[...], output_weights()).astype(BF16)
    c_wq.arrive()
    project_query(mid_b[...])
    for g in side_a:
        g.step(2)
    mix_grads((0, 1))
    for g in side_a:
        g.step(3)
    for g in g_x:
        g.step(0)
    mix_grads((2, 3))
    attend_grads()
    for g in g_d:
        g.begin()
    c_d.step(0)
    c_x.begin_line()
    sections.terms_begin()
    for g in side_a:
        g.step(4)
    c_d.step(1)

    for g in g_x:
        g.step(1)
    c_a.arrive()
    c_d.step(2)
    lax.fori_loop(0, 2, expert_forward, 0)
    for g in g_x:
        g.step(2)
    c_d.step(3)
    lax.fori_loop(2, 4, expert_forward, 0)
    for g in g_x:
        g.step(3)
    for g in g_d:
        g.step(0)
    c_d.step(4)
    c_d.begin_line()
    lax.fori_loop(4, 6, expert_forward, 0)
    for g in g_x:
        g.step(4)
    lax.fori_loop(6, 8, expert_forward, 0)
    cross_a.begin()

    for s in range(1, 4):
        for g in g_d:
            g.step(s)
        if s == 1:
            c_x.arrive()
            sections.terms_sum()
        lax.fori_loop((0, 0, 2, 5)[s], (0, 2, 5, 8)[s], expert_slopes, 0)
    scatter_a.step(0)
    for g in g_d:
        g.step(4)

    for s in range(1, 4):
        scatter_a.step(s)
        if s == 1:
            c_d.arrive()
            cross_a.sum_line()
        cross_a.step(s - 1)
        lax.fori_loop((0, 0, 3, 6)[s], (0, 3, 6, 8)[s], expert_backward, 0)
    cross_b.begin()
    scatter_b.step(0)
    cross_a.step(3)
    scatter_a.cross()
    cross_a.step(4)

    scatter_b.step(1)
    mixed_a = jnp.concatenate([scatter_a.total(), cross_a.total()], axis=1)
    middle[...] = (hidden_a[...].astype(F32) + mixed_a).astype(BF16)
    sections.spread_root(middle)
    sections.spread_leader()
    scatter_b.step(2)
    sections.spread_wait()
    project_query(middle[...])
    project_memory(memory[...])
    cross_b.sum_line()
    cross_b.step(0)
    allowed = allowed_keys(lengths[0, 0], lengths[1, 0])
    for p in range(INNER // PAIR):
        at = slice(p * PAIR, (p + 1) * PAIR)
        mixed[:, at] = mix_pair(query[:, at], key[:, at], value[:, at], allowed)
    scatter_b.step(3)
    cross_b.step(1)
    projected = jnp.where(is_decoder, dot_nn(mixed[...], output_weights()), 0.0)
    out_rows[...] = (middle[...].astype(F32) + projected).astype(BF16)
    ahead = sections.passing(out_rows, rows_out, 1, 0)
    ahead.start()
    cross_b.step(2)
    cross_b.step(3)
    scatter_b.cross()
    cross_b.step(4)
    sections.terms_finish()
    for g in weights + side_a + g_x + g_d + crosses + [c_d]:
        g.finish()
    scatter_a.finish()
    cross_a.finish()
    sections.spread_finish()
    back = jnp.concatenate([scatter_b.total(), cross_b.total()], axis=1)
    through = norm_grad(hidden_b[...], gain_moe, back)
    grad_rows[...] = (upstream[...].astype(F32) + through).astype(BF16)
    behind = sections.passing(grad_rows, grads_out, -1, 1)
    behind.start()
    scatter_b.finish()
    cross_b.finish()
    ahead.wait()
    behind.wait()


def on_device(
    hidden_fwd,
    hidden_bwd,
    mid_bwd,
    grads_in,
    memory_saved,
    lengths,
    routes_fwd,
    routes_bwd,
    probs_fwd,
    probs_bwd,
    norm_gains,
    w_in,
    w_out,
    w_query,
    w_keyval,
    w_output,
):
    shape = jax.ShapeDtypeStruct((TOK, D), BF16)
    vmem = pl.BlockSpec(memory_space=pltpu.VMEM)
    smem = pl.BlockSpec(memory_space=pltpu.SMEM)
    row_buf = pltpu.VMEM((NZ, NY, TOK, D), BF16)
    tok_buf = pltpu.VMEM((TOK, D), BF16)
    inner_buf = pltpu.VMEM((TOK, INNER), BF16)
    passed_rows, passed_grads, memory_grad = pl.pallas_call(
        kernel,
        out_shape=[shape] * 3,
        in_specs=[vmem] * 5 + [smem] + [vmem] * 10,
        out_specs=[vmem] * 3,
        scratch_shapes=[
            pltpu.VMEM((NZ, NY, 32, INNER), BF16),
            pltpu.VMEM((NZ, NY, 32, 2 * INNER), BF16),
            pltpu.VMEM((NZ, NY, 16, D), BF16),
            pltpu.VMEM((NZ, NY, 8, 128), F32),
            row_buf,
            row_buf,
            row_buf,
            row_buf,
            row_buf,
            pltpu.VMEM((NZ, LINE, UNITS), F32),
            inner_buf,
            inner_buf,
            inner_buf,
            inner_buf,
            tok_buf,
            tok_buf,
            tok_buf,
            tok_buf,
            tok_buf,
            tok_buf,
            pltpu.VMEM((NSEC - 1, PIECE_ROWS, PIECE_COLS), BF16),
        ]
        + GATHER_SEMS * 14
        + scatter_scratch(CUT_RA)
        + scatter_scratch(CUT_RB)
        + cross_scratch(CUT_RA)
        + cross_scratch(CUT_RB)
        + [
            pltpu.SemaphoreType.DMA((6,)),
            pltpu.SemaphoreType.DMA,
            pltpu.SemaphoreType.DMA((NSEC - 1,)),
            pltpu.SemaphoreType.DMA((NSEC - 1,)),
            pltpu.SemaphoreType.DMA((NSEC - 1,)),
            pltpu.SemaphoreType.DMA((NSEC - 1,)),
            pltpu.SemaphoreType.DMA((2,)),
            pltpu.SemaphoreType.DMA((2,)),
        ],
        compiler_params=pltpu.CompilerParams(
            collective_id=0, has_side_effects=True, vmem_limit_bytes=56 * 2**20
        ),
        name="relay_step",
    )(
        hidden_fwd[0],
        hidden_bwd[0],
        mid_bwd[0],
        grads_in[0],
        memory_saved,
        lengths.T,
        routes_fwd[0].T,
        routes_bwd[0].T,
        probs_fwd[0].T,
        probs_bwd[0].T,
        norm_gains[0],
        w_in[0],
        w_out[0],
        w_query[0],
        w_keyval[0],
        w_output[0],
    )
    return (passed_rows[None], passed_grads[None], memory_grad)


def solution(mesh):
    return jax.shard_map(
        on_device,
        mesh=mesh,
        in_specs=(
            P("section", "expert", None),
            P("section", "expert", None),
            P("section", "expert", None),
            P("section", "expert", None),
            P("expert", None),
            P(None, "expert"),
            P("section", "expert", None),
            P("section", "expert", None),
            P("section", "expert", None),
            P("section", "expert", None),
            P("section", None, None),
            P("section", None, "expert"),
            P("section", "expert", None),
            P("section", "expert", None),
            P("section", "expert", None),
            P("section", "expert", None),
        ),
        out_specs=(P("section", "expert", None), P("section", "expert", None), P("expert", None)),
        check_vma=False,
    )
```

```python
import functools

import jax
import jax.numpy as jnp
from jax import lax
from jax.experimental import pallas as pl
from jax.experimental.pallas import tpu as pltpu
from jax.sharding import PartitionSpec as P

MESH = pl.DeviceIdType.MESH
BF16 = jnp.bfloat16
F32 = jnp.float32
HEAD_DIM = 64
EXPERTS = 4
SEQ = 32
NZ = 8
NY = 4
NSEC = 16
FIRST_DECODER = 3
ROOT = FIRST_DECODER - 1
TOK = 64
LINE = NY * TOK
D = 1024
CUT_A, CUT_X, CUT_D, CUT_RA, CUT_RB = 768, 768, 768, 768, 768
UNITS = 512
INNER = 512
PAIR = 2 * HEAD_DIM

EPS = 1e-05
ROOT_HALF = 0.7071067811865476
INV_ROOT_TWO_PI = 0.3989422804014327


def dot_nn(a, b):
    return lax.dot_general(a, b, (((1,), (0,)), ((), ())), preferred_element_type=F32)


def dot_nt(a, b):
    return lax.dot_general(a, b, (((1,), (1,)), ((), ())), preferred_element_type=F32)


def dot_tn(a, b):
    return lax.dot_general(a, b, (((0,), (0,)), ((), ())), preferred_element_type=F32)


def norm_parts(row_block):
    values = row_block.astype(F32)
    center = values - jnp.mean(values, axis=-1, keepdims=True)
    spread = jnp.mean(center * center, axis=-1, keepdims=True)
    scale = lax.rsqrt(spread + EPS)
    return center * scale, scale


def norm_rows(row_block, gain_row):
    return (norm_parts(row_block)[0] * gain_row).astype(BF16)


def norm_grad(row_block, gain_row, upstream):
    unit, scale = norm_parts(row_block)
    grad = upstream * gain_row
    mean_grad = jnp.mean(grad, axis=-1, keepdims=True)
    mean_along = jnp.mean(grad * unit, axis=-1, keepdims=True)
    return scale * (grad - mean_grad - unit * mean_along)


def gelu_value(inputs):
    return 0.5 * inputs * (1.0 + lax.erf(inputs * ROOT_HALF))


def gelu_slope(inputs):
    return (
        0.5 * (1.0 + lax.erf(inputs * ROOT_HALF))
        + inputs * jnp.exp(-0.5 * inputs * inputs) * INV_ROOT_TWO_PI
    )


def allowed_keys(len_first, len_second):
    row = lax.broadcasted_iota(jnp.int32, (TOK, TOK), 0)
    col = lax.broadcasted_iota(jnp.int32, (TOK, TOK), 1)
    col_len = jnp.where(col < SEQ, len_first, len_second)
    same = (row < SEQ) == (col < SEQ)
    return same & (jnp.where(col < SEQ, col, col - SEQ) < col_len)


def live_row(len_first, len_second):
    col = lax.broadcasted_iota(jnp.int32, (1, TOK), 1)
    col_len = jnp.where(col < SEQ, len_first, len_second)
    return jnp.where(jnp.where(col < SEQ, col, col - SEQ) < col_len, 1.0, 0.0)


def one_head(values, side):
    lane = lax.broadcasted_iota(jnp.int32, values.shape, 1)
    return jnp.where((lane < HEAD_DIM) == (side == 0), values, jnp.zeros_like(values))


def head_weights(query, key, allowed):
    scores = dot_nt(query, key) * HEAD_DIM ** (-0.5)
    raised = jnp.where(allowed, jnp.exp(scores), 0.0)
    return raised / jnp.sum(raised, axis=-1, keepdims=True)


def mix_pair(query, key, value, allowed):
    mixed = jnp.zeros((TOK, PAIR), F32)
    for side in (0, 1):
        weights = head_weights(one_head(query, side), key, allowed).astype(BF16)
        mixed = mixed + dot_nn(weights, one_head(value, side))
    return mixed.astype(BF16)


def mix_pair_grad(query, key, value, d_mixed, allowed):
    d_query = jnp.zeros((TOK, PAIR), F32)
    d_key = jnp.zeros((TOK, PAIR), F32)
    d_value = jnp.zeros((TOK, PAIR), F32)
    for side in (0, 1):
        query_one, grad_one = one_head(query, side), one_head(d_mixed, side)
        exact = head_weights(query_one, key, allowed)
        d_weights = dot_nt(grad_one, value).astype(BF16).astype(F32)
        d_value = d_value + dot_tn(exact.astype(BF16), grad_one)
        along = jnp.sum(d_weights * exact, axis=-1, keepdims=True)
        d_scores = (exact * (d_weights - along) * HEAD_DIM ** (-0.5)).astype(BF16)
        d_query = d_query + dot_nn(d_scores, one_head(key, side))
        d_key = d_key + dot_tn(d_scores, query_one)
    return d_query.astype(BF16), d_key.astype(BF16), d_value.astype(BF16)


def upright(row):
    eye = lax.broadcasted_iota(jnp.int32, (TOK, TOK), 0) == lax.broadcasted_iota(
        jnp.int32, (TOK, TOK), 1
    )
    return jnp.sum(jnp.where(eye, row, 0.0), axis=1, keepdims=True)


def place():
    me = lax.axis_index("expert")
    return me, lax.div(me, NY), lax.rem(me, NY)


def to_expert(z, y):
    return {"expert": lax.rem(z + 2 * NZ, NZ) * NY + lax.rem(y + 2 * NY, NY)}


def to_section(s):
    return {"section": lax.rem(s + 2 * NSEC, NSEC)}


def remote(src, dst, send, recv, device):
    return pltpu.make_async_remote_copy(
        src_ref=src, dst_ref=dst, send_sem=send, recv_sem=recv, device_id=device, device_id_type=MESH
    )


class Ring:
    def __init__(self, view, send, recv):
        self.view, self.send, self.recv = view, send, recv
        _, self.z, self.y = place()

    def hop(self, way, step, arriving):
        sign = 1 if way == 0 else -1
        back = step + 1 if arriving else step
        origin = lax.rem(self.z - sign * back + 2 * NZ, NZ)
        block = self.view(origin, way if step == 3 else None)
        return remote(
            block, block, self.send.at[way, step], self.recv.at[way, step], to_expert(self.z + sign, self.y)
        )

    def step(self, s):
        for way in (0, 1):
            if s > 0:
                self.hop(way, s - 1, True).wait_recv()
            if s < 4:
                self.hop(way, s, False).start()

    def finish(self):
        for way in (0, 1):
            for s in range(4):
                self.hop(way, s, False).wait_send()


class Line:
    def __init__(self, view, send, recv):
        self.view, self.send, self.recv = view, send, recv
        _, self.z, self.y = place()

    def copy(self, d, arriving):
        block = self.view(lax.rem(self.y + NY - d, NY) if arriving else self.y)
        return remote(block, block, self.send.at[d - 1], self.recv.at[d - 1], to_expert(self.z, self.y + d))

    def begin(self):
        for d in (1, 2, 3):
            self.copy(d, False).start()

    def arrive(self):
        for d in (1, 2, 3):
            self.copy(d, True).wait_recv()

    def finish(self):
        for d in (1, 2, 3):
            self.copy(d, False).wait_send()


class RelayLine(Line):
    def inner(self):
        return (self.y == 1) | (self.y == 2)

    def begin(self):
        for d in (1, 3):
            self.copy(d, False).start()

        @pl.when(jnp.logical_not(self.inner()))
        def _():
            self.copy(2, False).start()

    def relay(self):
        @pl.when(self.y == 1)
        def _():
            self.copy(3, True).wait_recv()

        @pl.when(self.y == 2)
        def _():
            self.copy(1, True).wait_recv()

        @pl.when(self.inner())
        def _():
            block = self.view(NY - 1 - self.y)
            target = to_expert(self.z, jnp.where(self.y == 1, 0, NY - 1))
            remote(block, block, self.send.at[1], self.recv.at[1], target).start()

    def arrive(self):
        self.copy(2, True).wait_recv()

        @pl.when(self.y != 2)
        def _():
            self.copy(1, True).wait_recv()

        @pl.when(self.y != 1)
        def _():
            self.copy(3, True).wait_recv()


def halves(cut):
    first = (cut // 128 + 1) // 2 * 128
    return (0, first), (first, cut - first)


class Gather:
    def __init__(self, array, first_col, cols, ysend, yrecv, zsend, zrecv):
        _, z, _ = place()
        at = pl.ds(first_col, cols)
        self.line = Line(lambda y: array.at[z, y, :, at], ysend, yrecv)

        def view(origin, half):
            if half is None:
                return array.at[origin, :, :, at]
            return array.at[origin, pl.ds(half * 2, 2), :, at]

        self.ring = Ring(view, zsend, zrecv)

    def begin(self):
        self.line.begin()

    def step(self, s):
        if s == 0:
            self.line.arrive()
        self.ring.step(s)

    def finish(self):
        self.line.finish()
        self.ring.finish()


class CrossGather:
    def __init__(self, array, first_col, cols, ysend, yrecv, zsend, zrecv):
        _, _, me_y = place()
        at = pl.ds(first_col, cols)
        rows = array.shape[2] // 2

        def view(origin, half):
            if half is None:
                return array.at[origin, me_y, :, at]
            return array.at[origin, me_y, pl.ds(half * rows, rows), at]

        self.ring = Ring(view, zsend, zrecv)
        self.line = RelayLine(lambda y: array.at[:, y, :, at], ysend, yrecv)

    def step(self, s):
        self.ring.step(s)

    def begin_line(self):
        self.line.begin()

    def relay(self):
        self.line.relay()

    def arrive(self):
        self.line.arrive()

    def finish(self):
        self.ring.finish()
        self.line.finish()


GATHER_SEMS = [
    pltpu.SemaphoreType.DMA((3,)),
    pltpu.SemaphoreType.DMA((3,)),
    pltpu.SemaphoreType.DMA((2, 4)),
    pltpu.SemaphoreType.DMA((2, 4)),
]


class SumRing:
    def __init__(self, own, slot, send, recv):
        self.own, self.slot, self.send, self.recv = own, slot, send, recv
        _, self.z, self.y = place()

    def term(self, way, step, chunk):
        sign = 1 if way == 0 else -1
        return self.own(lax.rem(self.z + sign * (4 - step) + 2 * NZ, NZ), chunk)

    def hop(self, way, step, chunk):
        first = 0 if chunk == way else 1
        source = self.term(way, step, chunk) if step == first else self.slot(way, step - 1, chunk)
        return remote(
            source,
            self.slot(way, step, chunk),
            self.send.at[way, step, chunk],
            self.recv.at[way, step, chunk],
            to_expert(self.z + (1 if way == 0 else -1), self.y),
        )

    def step(self, s, chunks=(0, 1)):
        for chunk in chunks:
            for way in (0, 1):
                first = 0 if chunk == way else 1
                if s < first:
                    continue
                if s > first:
                    self.hop(way, s - 1, chunk).wait_recv()
                    if s < 4:
                        slot = self.slot(way, s - 1, chunk)
                        slot[...] = (
                            slot[...].astype(F32) + self.term(way, s, chunk)[...].astype(F32)
                        ).astype(BF16)
                if s < 4:
                    self.hop(way, s, chunk).start()

    def total(self, chunk):
        return (
            self.own(self.z, chunk)[...].astype(F32)
            + self.slot(0, 3, chunk)[...].astype(F32)
            + self.slot(1, 3, chunk)[...].astype(F32)
        )

    def finish(self):
        for chunk in (0, 1):
            for way in (0, 1):
                for s in range(0 if chunk == way else 1, 4):
                    self.hop(way, s, chunk).wait_send()


class SumLine:
    def __init__(self, src, slot, send, recv):
        self.src, self.slot, self.send, self.recv = src, slot, send, recv
        _, self.z, self.y = place()

    def copy(self, d, chunk):
        return remote(
            self.src(lax.rem(self.y + d, NY), chunk),
            self.slot(d, chunk),
            self.send.at[chunk, d - 1],
            self.recv.at[chunk, d - 1],
            to_expert(self.z, self.y + d),
        )

    def begin(self, chunk):
        for d in (1, 2, 3):
            self.copy(d, chunk).start()

    def arrive(self, chunk):
        for d in (1, 2, 3):
            self.copy(d, chunk).wait_recv()

    def finish(self):
        for chunk in (0, 1):
            for d in (1, 2, 3):
                self.copy(d, chunk).wait_send()


class DirectSum:
    def __init__(self, src, slots, send, recv):
        self.src, self.slots, self.send, self.recv = src, slots, send, recv
        _, self.z, self.y = place()

    def copy(self, d):
        return remote(
            self.src(lax.rem(self.y + d, NY)),
            self.slots.at[d - 1],
            self.send.at[d - 1],
            self.recv.at[d - 1],
            to_expert(self.z, self.y + d),
        )

    def begin(self):
        for d in (1, 2, 3):
            self.copy(d).start()

    def total(self, sums):
        for d in (1, 2, 3):
            self.copy(d).wait_recv()
        own = self.src(self.y)

        def add(block, _):
            result = own[block].astype(F32)
            for d in (1, 2, 3):
                result = result + self.slots[d - 1, block].astype(F32)
            sums[block] = result.astype(BF16)
            return 0

        lax.fori_loop(0, NZ, add, 0)

    def finish(self):
        for d in (1, 2, 3):
            self.copy(d).wait_send()


class Scatter:
    def __init__(self, cut, src, slots, line_buf, line_slots, zsend, zrecv, ysend, yrecv):
        def part(chunk):
            return pl.ds(chunk * SEQ, SEQ)

        at = pl.ds(0, cut)
        self.part, self.line_buf, self.line_slots = part, line_buf, line_slots
        self.ring = SumRing(
            lambda dest, chunk: src.at[dest, :, part(chunk), at],
            lambda way, step, chunk: slots.at[way, step, :, part(chunk)],
            zsend,
            zrecv,
        )
        self.line = SumLine(
            lambda y, chunk: line_buf.at[y, part(chunk)],
            lambda d, chunk: line_slots.at[d - 1, part(chunk)],
            ysend,
            yrecv,
        )

    def step(self, s):
        self.ring.step(s)

    def cross(self):
        for chunk in (0, 1):
            self.ring.step(4, (chunk,))
            self.line_buf[:, self.part(chunk)] = self.ring.total(chunk).astype(BF16)
            self.line.begin(chunk)

    def total(self, chunk):
        self.line.arrive(chunk)
        result = self.line_buf[self.line.y, self.part(chunk)].astype(F32)
        for d in (1, 2, 3):
            result = result + self.line_slots[d - 1, self.part(chunk)].astype(F32)
        return result

    def finish(self):
        self.ring.finish()
        self.line.finish()


class CrossScatter:
    def __init__(self, cut, src, line_slots, sums, slots, ysend, yrecv, zsend, zrecv):
        at = pl.ds(cut, D - cut)
        self.sums = sums
        self.line = DirectSum(lambda y: src.at[:, y, :, at], line_slots, ysend, yrecv)
        self.ring = SumRing(
            lambda dest, chunk: sums.at[dest, pl.ds(chunk * 32, 32)],
            lambda way, step, chunk: slots.at[way, step, pl.ds(chunk * 32, 32)],
            zsend,
            zrecv,
        )

    def begin(self):
        self.line.begin()

    def sum_line(self):
        self.line.total(self.sums)

    def step(self, s):
        self.ring.step(s)

    def total(self, chunk):
        return self.ring.total(chunk)

    def finish(self):
        self.line.finish()
        self.ring.finish()


def scatter_scratch(cut):
    return [
        pltpu.VMEM((2, 4, NY, TOK, cut), BF16),
        pltpu.VMEM((NY, TOK, cut), BF16),
        pltpu.VMEM((3, TOK, cut), BF16),
    ] + [pltpu.SemaphoreType.DMA(dims) for dims in ((2, 4, 2), (2, 4, 2), (2, 3), (2, 3))]


def cross_scratch(cut):
    return [
        pltpu.VMEM((3, NZ, TOK, D - cut), BF16),
        pltpu.VMEM((NZ, TOK, D - cut), BF16),
        pltpu.VMEM((2, 4, TOK, D - cut), BF16),
    ] + [pltpu.SemaphoreType.DMA(dims) for dims in ((3,), (3,), (2, 4, 2), (2, 4, 2))]


PIECE_ROWS = 32
PIECE_COLS = 128


def piece(ref, index):
    row = pl.multiple_of(lax.div(index, 8) * PIECE_ROWS, PIECE_ROWS)
    col = pl.multiple_of(lax.rem(index, 8) * PIECE_COLS, PIECE_COLS)
    return ref.at[pl.ds(row, PIECE_ROWS), pl.ds(col, PIECE_COLS)]


class Sections:
    def __init__(self, memory, term_rows, terms, total, bsend, brecv, tsend, trecv, gsend, grecv, psend, precv):
        self.memory, self.term_rows, self.terms, self.sum_rows = memory, term_rows, terms, total
        self.bsend, self.brecv, self.tsend, self.trecv = bsend, brecv, tsend, trecv
        self.gsend, self.grecv, self.psend, self.precv = gsend, grecv, psend, precv
        self.s = lax.axis_index("section")
        self.is_root = self.s == ROOT
        self.is_leader = lax.rem(self.s, 4) == ROOT % 4

    def spread(self, slot, d):
        return remote(self.memory, self.memory, self.bsend.at[slot], self.brecv, to_section(self.s + d))

    def spread_root(self, middle):
        @pl.when(self.is_root)
        def _():
            self.memory[...] = middle[...]
            for slot in (0, 1, 2):
                self.spread(slot, 4 * (slot + 1)).start()

    def spread_leader(self):
        @pl.when(self.is_leader & jnp.logical_not(self.is_root))
        def _():
            self.spread(0, 4).wait_recv()

        @pl.when(self.is_leader)
        def _():
            for slot, d in ((3, -2), (4, -1), (5, 1)):
                self.spread(slot, d).start()

    def spread_wait(self):
        @pl.when(jnp.logical_not(self.is_leader))
        def _():
            self.spread(0, 4).wait_recv()

    def spread_finish(self):
        @pl.when(self.is_root)
        def _():
            for slot in (0, 1, 2):
                self.spread(slot, 4).wait_send()

        @pl.when(self.is_leader)
        def _():
            for slot in (3, 4, 5):
                self.spread(slot, 1).wait_send()

    def term(self, d):
        target = lax.rem(self.s + d, NSEC)
        return remote(
            piece(self.term_rows, target),
            self.terms.at[d - 1],
            self.tsend.at[d - 1],
            self.trecv.at[d - 1],
            to_section(self.s + d),
        )

    def terms_begin(self):
        for d in range(1, NSEC):
            self.term(d).start()

    def result(self, d, arriving):
        index = lax.rem(self.s + NSEC - d, NSEC) if arriving else self.s
        view = piece(self.sum_rows, index)
        return remote(view, view, self.gsend.at[d - 1], self.grecv.at[d - 1], to_section(self.s + d))

    def terms_sum(self):
        own = piece(self.term_rows, self.s)[...].astype(F32)
        for d in range(1, NSEC):
            self.term(d).wait_recv()
            own = own + self.terms[d - 1].astype(F32)
        view = piece(self.sum_rows, self.s)
        view[...] = own.astype(BF16)
        for d in range(1, NSEC):
            self.result(d, False).start()

    def terms_finish(self):
        for d in range(1, NSEC):
            self.result(d, True).wait_recv()
        for d in range(1, NSEC):
            self.term(d).wait_send()
            self.result(d, False).wait_send()

    def passing(self, src, dst, d, slot):
        return remote(src, dst, self.psend.at[slot], self.precv.at[slot], to_section(self.s + d))


def kernel(
    hidden_a, hidden_b, mid_b, cotangent, mem_saved, lengths,
    routes_f, routes_b, probs_f, probs_b, gains, w_in, w_out, w_query, w_keyval, w_output,
    rows_out, grads_out, memory_grad_out,
    all_query, all_keyval, all_output, all_shares, all_a, all_x, all_d, part_a, part_b, slopes,
    query, key, value, mixed, middle, upstream, out_rows, grad_rows,
    memory, term_rows, terms, *sems
):
    sems = list(sems)

    def take(count):
        taken = sems[:count]
        del sems[:count]
        return taken

    me, z, y = place()
    my_expert = lax.div(me, NZ)
    section = lax.axis_index("section")
    is_decoder = section >= FIRST_DECODER
    gain_moe = gains[0:1, :]
    gain_att = gains[1:2, :]

    g_wo = Gather(all_output, 0, D, *take(4))
    g_wkv = [Gather(all_keyval, c * INNER, INNER, *take(4)) for c in (0, 1)]
    g_sh = Gather(all_shares, 0, 128, *take(4))
    g_a = [Gather(all_a, *at, *take(4)) for at in halves(CUT_A)]
    g_x = [Gather(all_x, *at, *take(4)) for at in halves(CUT_X)]
    g_d = [Gather(all_d, *at, *take(4)) for at in halves(CUT_D)]
    c_wq = CrossGather(all_query, 0, INNER, *take(4))
    c_a = CrossGather(all_a, CUT_A, D - CUT_A, *take(4))
    c_x = CrossGather(all_x, CUT_X, D - CUT_X, *take(4))
    c_d = CrossGather(all_d, CUT_D, D - CUT_D, *take(4))
    scatter_a = Scatter(CUT_RA, part_a, *take(7))
    scatter_b = Scatter(CUT_RB, part_b, *take(7))
    cross_a = CrossScatter(CUT_RA, part_a, *take(7))
    cross_b = CrossScatter(CUT_RB, part_b, *take(7))
    sections = Sections(memory, term_rows, terms, memory_grad_out, *take(8))

    partners = (
        [to_expert(z + 1, y), to_expert(z - 1, y)]
        + [to_expert(z, y + d) for d in (1, 2, 3)]
        + [to_section(section + d) for d in range(1, NSEC)]
    )
    barrier = pltpu.get_barrier_semaphore()
    for device in partners:
        pl.semaphore_signal(barrier, inc=1, device_id=device, device_id_type=MESH)

    all_output[z, y] = w_output[...]
    all_query[z, y] = w_query[...]
    all_keyval[z, y] = w_keyval[...]
    pl.semaphore_wait(barrier, len(partners))

    def share_column(block, i, base):
        return upright(all_shares[block, i, pl.ds(base + my_expert, 1), 0:TOK])

    def line_rows(ref, block):
        return ref[block].reshape(LINE, D)

    def expert_forward(block, _):
        units = gelu_value(dot_nn(line_rows(all_a, block), w_in[...])).astype(BF16)
        part = dot_nn(units, w_out[...])
        for i in range(NY):
            share = share_column(block, i, 0)
            part_a[block, i] = (part[i * TOK : (i + 1) * TOK] * share).astype(BF16)
        return 0

    def expert_slopes(block, _):
        slopes[block] = gelu_slope(dot_nn(line_rows(all_x, block), w_in[...]))
        return 0

    def expert_backward(block, _):
        for i in range(NY):
            part_b[block, i] = (all_d[block, i].astype(F32) * share_column(block, i, 4)).astype(BF16)
        unit_grad = (dot_nt(line_rows(part_b, block), w_out[...]) * slopes[block]).astype(BF16)
        part_b[block] = dot_nt(unit_grad, w_in[...]).astype(BF16).reshape(NY, TOK, D)
        return 0

    def query_weights():
        return all_query[...].reshape(D, INNER)

    def keyval_weights(first):
        return all_keyval[:, :, :, first : first + INNER].reshape(D, INNER)

    def output_weights():
        return all_output[...].reshape(INNER, D)

    def project_memory(mem_rows):
        key[...] = dot_nn(mem_rows, keyval_weights(0)).astype(BF16)
        value[...] = dot_nn(mem_rows, keyval_weights(INNER)).astype(BF16)

    def project_query(mid_rows):
        query[...] = dot_nn(norm_rows(mid_rows, gain_att), query_weights()).astype(BF16)

    def mix_grads(pairs):
        allowed = allowed_keys(lengths[0, 2], lengths[1, 2])
        for p in pairs:
            at = slice(p * PAIR, (p + 1) * PAIR)
            grads = mix_pair_grad(query[:, at], key[:, at], value[:, at], mixed[:, at], allowed)
            query[:, at], key[:, at], value[:, at] = grads

    def attend_grads():
        d_normed = dot_nt(query[...], query_weights()).astype(BF16).astype(F32)
        d_memory = dot_nt(key[...], keyval_weights(0)) + dot_nt(value[...], keyval_weights(INNER))
        term_rows[...] = jnp.where(is_decoder, d_memory, 0.0).astype(BF16)
        through = norm_grad(mid_b[...], gain_att, d_normed).astype(BF16).astype(F32)
        cot = cotangent[...].astype(F32)
        upstream[...] = jnp.where(is_decoder, cot + through, cot).astype(BF16)
        all_d[z, y] = upstream[...]

    weights, side_a = [g_wo] + g_wkv, [g_sh] + g_a
    crosses = [c_wq, c_a, c_x]

    for g in weights:
        g.begin()
    c_wq.step(0)
    all_a[z, y] = norm_rows(hidden_a[...], gain_moe)
    all_x[z, y] = norm_rows(hidden_b[...], gain_moe)
    own_shares = all_shares.at[z, y]
    own_shares[...] = jnp.zeros((8, 128), F32)
    for base, routes, probs, line in ((0, routes_f, probs_f, 0), (4, routes_b, probs_b, 2)):
        live = live_row(
            jnp.where(is_decoder, lengths[0, line + 1], lengths[0, line]),
            jnp.where(is_decoder, lengths[1, line + 1], lengths[1, line]),
        )
        for e in range(EXPERTS):
            share = jnp.where(routes[0:1, :] == e, probs[0:1, :], 0.0) + jnp.where(
                routes[1:2, :] == e, probs[1:2, :], 0.0
            )
            own_shares[base + e : base + e + 1, 0:TOK] = share * live
    for g in side_a:
        g.begin()
    c_a.step(0)
    c_x.step(0)
    for s in range(1, 5):
        if s < 4:
            weights[s - 1].step(0)
        for c in crosses:
            c.step(s)
    for g in weights:
        g.step(1)
    c_wq.begin_line()
    for g in weights:
        g.step(2)
    for g in g_x:
        g.begin()
    c_a.begin_line()
    for g in weights:
        g.step(3)
    for g in side_a:
        g.step(0)
    for g in weights:
        g.step(4)
    c_wq.relay()

    for g in side_a:
        g.step(1)
    project_memory(mem_saved[...])
    mixed[...] = dot_nt(cotangent[...], output_weights()).astype(BF16)
    c_wq.arrive()
    project_query(mid_b[...])
    for g in side_a:
        g.step(2)
    c_a.relay()
    mix_grads((0, 1))
    for g in side_a:
        g.step(3)
    for g in g_x:
        g.step(0)
    mix_grads((2, 3))
    attend_grads()
    for g in g_d:
        g.begin()
    c_d.step(0)
    c_x.begin_line()
    sections.terms_begin()
    for g in side_a:
        g.step(4)
    c_d.step(1)

    for g in g_x:
        g.step(1)
    c_a.arrive()
    c_d.step(2)
    lax.fori_loop(0, 2, expert_forward, 0)
    for g in g_x:
        g.step(2)
    c_x.relay()
    c_d.step(3)
    lax.fori_loop(2, 4, expert_forward, 0)
    for g in g_x:
        g.step(3)
    for g in g_d:
        g.step(0)
    c_d.step(4)
    c_d.begin_line()
    lax.fori_loop(4, 6, expert_forward, 0)
    for g in g_x:
        g.step(4)
    lax.fori_loop(6, 8, expert_forward, 0)

    for s in range(1, 4):
        for g in g_d:
            g.step(s)
        if s == 1:
            c_x.arrive()
            sections.terms_sum()
        if s == 2:
            c_d.relay()
        if s == 3:
            cross_a.begin()
        lax.fori_loop((0, 0, 2, 5)[s], (0, 2, 5, 8)[s], expert_slopes, 0)
    scatter_a.step(0)
    for g in g_d:
        g.step(4)

    for s in range(1, 4):
        scatter_a.step(s)
        if s == 1:
            c_d.arrive()
        lax.fori_loop((0, 0, 3, 6)[s], (0, 3, 6, 8)[s], expert_backward, 0)
    scatter_b.step(0)
    cross_a.sum_line()
    cross_a.step(0)
    scatter_a.cross()
    cross_b.begin()
    cross_a.step(1)

    scatter_b.step(1)
    for s in (2, 3, 4):
        cross_a.step(s)
    for chunk in (0, 1):
        part = pl.ds(chunk * SEQ, SEQ)
        mixed_a = jnp.concatenate([scatter_a.total(chunk), cross_a.total(chunk)], axis=1)
        middle[part] = (hidden_a[part].astype(F32) + mixed_a).astype(BF16)
    sections.spread_root(middle)
    scatter_b.step(2)
    sections.spread_leader()
    project_query(middle[...])
    cross_b.sum_line()
    cross_b.step(0)
    scatter_b.step(3)
    sections.spread_wait()
    project_memory(memory[...])
    cross_b.step(1)
    allowed = allowed_keys(lengths[0, 0], lengths[1, 0])
    for p in range(INNER // PAIR):
        at = slice(p * PAIR, (p + 1) * PAIR)
        mixed[:, at] = mix_pair(query[:, at], key[:, at], value[:, at], allowed)
    cross_b.step(2)
    projected = jnp.where(is_decoder, dot_nn(mixed[...], output_weights()), 0.0)
    out_rows[...] = (middle[...].astype(F32) + projected).astype(BF16)
    ahead = sections.passing(out_rows, rows_out, 1, 0)
    ahead.start()
    cross_b.step(3)
    scatter_b.cross()
    cross_b.step(4)
    sections.terms_finish()
    for g in weights + side_a + g_x + g_d + crosses + [c_d]:
        g.finish()
    scatter_a.finish()
    cross_a.finish()
    sections.spread_finish()
    behind = []
    for chunk in (0, 1):
        part = pl.ds(chunk * SEQ, SEQ)
        back = jnp.concatenate([scatter_b.total(chunk), cross_b.total(chunk)], axis=1)
        through = norm_grad(hidden_b[part], gain_moe, back)
        grad_rows[part] = (upstream[part].astype(F32) + through).astype(BF16)
        behind.append(sections.passing(grad_rows.at[part], grads_out.at[part], -1, 1 + chunk))
        behind[chunk].start()
    scatter_b.finish()
    cross_b.finish()
    ahead.wait()
    for copy in behind:
        copy.wait()


def on_device(
    hidden_fwd,
    hidden_bwd,
    mid_bwd,
    grads_in,
    memory_saved,
    lengths,
    routes_fwd,
    routes_bwd,
    probs_fwd,
    probs_bwd,
    norm_gains,
    w_in,
    w_out,
    w_query,
    w_keyval,
    w_output,
):
    shape = jax.ShapeDtypeStruct((TOK, D), BF16)
    vmem = pl.BlockSpec(memory_space=pltpu.VMEM)
    smem = pl.BlockSpec(memory_space=pltpu.SMEM)
    row_buf = pltpu.VMEM((NZ, NY, TOK, D), BF16)
    tok_buf = pltpu.VMEM((TOK, D), BF16)
    inner_buf = pltpu.VMEM((TOK, INNER), BF16)
    passed_rows, passed_grads, memory_grad = pl.pallas_call(
        kernel,
        out_shape=[shape] * 3,
        in_specs=[vmem] * 5 + [smem] + [vmem] * 10,
        out_specs=[vmem] * 3,
        scratch_shapes=[
            pltpu.VMEM((NZ, NY, 32, INNER), BF16),
            pltpu.VMEM((NZ, NY, 32, 2 * INNER), BF16),
            pltpu.VMEM((NZ, NY, 16, D), BF16),
            pltpu.VMEM((NZ, NY, 8, 128), F32),
            row_buf,
            row_buf,
            row_buf,
            row_buf,
            row_buf,
            pltpu.VMEM((NZ, LINE, UNITS), F32),
            inner_buf,
            inner_buf,
            inner_buf,
            inner_buf,
            tok_buf,
            tok_buf,
            tok_buf,
            tok_buf,
            tok_buf,
            tok_buf,
            pltpu.VMEM((NSEC - 1, PIECE_ROWS, PIECE_COLS), BF16),
        ]
        + GATHER_SEMS * 14
        + scatter_scratch(CUT_RA)
        + scatter_scratch(CUT_RB)
        + cross_scratch(CUT_RA)
        + cross_scratch(CUT_RB)
        + [
            pltpu.SemaphoreType.DMA((6,)),
            pltpu.SemaphoreType.DMA,
            pltpu.SemaphoreType.DMA((NSEC - 1,)),
            pltpu.SemaphoreType.DMA((NSEC - 1,)),
            pltpu.SemaphoreType.DMA((NSEC - 1,)),
            pltpu.SemaphoreType.DMA((NSEC - 1,)),
            pltpu.SemaphoreType.DMA((3,)),
            pltpu.SemaphoreType.DMA((3,)),
        ],
        compiler_params=pltpu.CompilerParams(
            collective_id=0, has_side_effects=True, vmem_limit_bytes=56 * 2**20
        ),
        name="relay_step",
    )(
        hidden_fwd[0],
        hidden_bwd[0],
        mid_bwd[0],
        grads_in[0],
        memory_saved,
        lengths.T,
        routes_fwd[0].T,
        routes_bwd[0].T,
        probs_fwd[0].T,
        probs_bwd[0].T,
        norm_gains[0],
        w_in[0],
        w_out[0],
        w_query[0],
        w_keyval[0],
        w_output[0],
    )
    return (passed_rows[None], passed_grads[None], memory_grad)


def solution(mesh):
    return jax.shard_map(
        on_device,
        mesh=mesh,
        in_specs=(
            P("section", "expert", None),
            P("section", "expert", None),
            P("section", "expert", None),
            P("section", "expert", None),
            P("expert", None),
            P(None, "expert"),
            P("section", "expert", None),
            P("section", "expert", None),
            P("section", "expert", None),
            P("section", "expert", None),
            P("section", None, None),
            P("section", None, "expert"),
            P("section", "expert", None),
            P("section", "expert", None),
            P("section", "expert", None),
            P("section", "expert", None),
        ),
        out_specs=(P("section", "expert", None), P("section", "expert", None), P("expert", None)),
        check_vma=False,
    )
```
